256 devices in a mesh: dp: 4 (over z_hi), ctx: 64 (over z_lo, x, y, core).
Axes of the slice: x: 4, y: 4, z: 8 (z_hi: 4, z_lo: 2; z = z_hi * 2 + z_lo), core: 2. Of those that a mesh axis runs over, the one named last changes fastest.
Arguments:
- query_proj: bfloat16 [1024, 32768], P(None, ('dp', 'ctx')), may hold values from -6 to 6
- key_proj: bfloat16 [1024, 32768], P(None, ('dp', 'ctx')), may hold values from -6 to 6
- value_proj: bfloat16 [1024, 32768], P(None, ('dp', 'ctx')), may hold values from -6 to 6
- filter_taps: bfloat16 [1024, 32768], P(None, ('dp', 'ctx')), may hold values from -1.1 to 1.1
- grad_out: bfloat16 [1024, 32768], P(None, ('dp', 'ctx')), may hold values from -1.5 to 1.5
Outputs:
- grad_query: bfloat16 [1024, 32768], P(None, ('dp', 'ctx'))
- grad_key: bfloat16 [1024, 32768], P(None, ('dp', 'ctx'))
- grad_value: bfloat16 [1024, 32768], P(None, ('dp', 'ctx'))
- grad_filter: bfloat16 [1024, 32768], P(None, ('dp', 'ctx'))
The draws below stay inside these ranges and needn't reach their ends.
All inputs are finite; a program needn't handle non-finite values.
Results may differ from the reference program's by a relative error of at most 0.0058.
Values may be sent and summed in bfloat16 or wider, within the bound.
A program may use at most 64 MiB of HBM per device.

```python
import math
import jax
import jax.numpy as jnp
from jax import lax

CHANNELS = 1024
LENGTH = 32768


def draw_filter_taps(key, part):
    key = jax.random.fold_in(key, 7)
    life_key, noise_key = jax.random.split(key)
    lags = jnp.arange(LENGTH, dtype=jnp.float32)[None, :]
    lifetime = jnp.exp(jax.random.uniform(life_key, (CHANNELS, 1), jnp.float32, math.log(30.0), math.log(2.0 * LENGTH)))
    noise_draw = jnp.clip(jax.random.normal(noise_key, (CHANNELS, LENGTH), jnp.float32), -4.0, 4.0)
    taps = noise_draw * jnp.exp(-lags / lifetime) * jnp.sqrt(2.0 / lifetime)
    return taps.astype(jnp.bfloat16)


def shard_levels(stream_key, extent, pieces, low, largest):
    loudness = 1.0
    for dim, blocks in pieces:
        heights = jax.random.uniform(jax.random.fold_in(jax.random.fold_in(stream_key, 6), dim), (blocks,), jnp.float32, low / len(pieces), largest / len(pieces))
        loudness = loudness * jnp.repeat(jnp.exp(heights), extent[dim] // blocks).reshape((-1,) + (1,) * (len(extent) - 1 - dim))
    return loudness


def scatter_about(key, dims, spread, most, pieces=(), held_as=jnp.bfloat16):
    factor_of = shard_levels(key, dims, pieces, -0.22, 0.18) if pieces else 1.0
    values = jax.random.normal(key, dims, jnp.float32) * spread * factor_of
    return jnp.minimum(jnp.maximum(values, -most), most).astype(held_as)


def setup_inputs(seed: int = 0) -> dict:
    seeds = jax.random.split(jax.random.key(seed), 6)
    query_proj = scatter_about(seeds[0], (CHANNELS, LENGTH), 1.0, 6.0, ((1, 256),))
    key_proj = scatter_about(seeds[1], (CHANNELS, LENGTH), 1.0, 6.0, ((1, 256),))
    value_proj = scatter_about(seeds[2], (CHANNELS, LENGTH), 1.0, 6.0, ((1, 256),))
    filter_taps = draw_filter_taps(jax.random.fold_in(seeds[5], 71), 0)
    grad_out = scatter_about(seeds[4], (CHANNELS, LENGTH), 0.25, 1.5, ((1, 256),))
    return {"query_proj": query_proj, "key_proj": key_proj, "value_proj": value_proj, "filter_taps": filter_taps, "grad_out": grad_out}


def block_terms(packed):
    source_block, signal_block, taps_block = packed
    padded_length = 2 * LENGTH
    source_freq = jnp.fft.rfft(source_block.astype(jnp.float32), n=padded_length, axis=-1)
    signal_freq = jnp.fft.rfft(signal_block.astype(jnp.float32), n=padded_length, axis=-1)
    taps_freq = jnp.fft.rfft(taps_block.astype(jnp.float32), n=padded_length, axis=-1)
    convolved = jnp.fft.irfft(taps_freq * source_freq, n=padded_length, axis=-1)[:, :LENGTH]
    back_signal = jnp.fft.irfft(jnp.conj(taps_freq) * signal_freq, n=padded_length, axis=-1)[:, :LENGTH]
    taps_grad = jnp.fft.irfft(jnp.conj(source_freq) * signal_freq, n=padded_length, axis=-1)[:, :LENGTH]
    return (convolved.astype(jnp.bfloat16), back_signal.astype(jnp.bfloat16), taps_grad.astype(jnp.bfloat16))


def reference(query_proj, key_proj, value_proj, filter_taps, grad_out):
    source = (key_proj.astype(jnp.float32) * value_proj.astype(jnp.float32)).astype(jnp.bfloat16)
    signal = (grad_out.astype(jnp.float32) * query_proj.astype(jnp.float32)).astype(jnp.bfloat16)
    block_rows = min(CHANNELS, 64)

    def as_blocks(array):
        return array.reshape(CHANNELS // block_rows, block_rows, LENGTH)

    convolved, back_signal, taps_grad = lax.map(block_terms, (as_blocks(source), as_blocks(signal), as_blocks(filter_taps)))
    convolved = convolved.reshape(CHANNELS, LENGTH)
    back_signal = back_signal.reshape(CHANNELS, LENGTH)
    taps_grad = taps_grad.reshape(CHANNELS, LENGTH)
    grad_query = (grad_out.astype(jnp.float32) * convolved.astype(jnp.float32)).astype(jnp.bfloat16)
    grad_key = (back_signal.astype(jnp.float32) * value_proj.astype(jnp.float32)).astype(jnp.bfloat16)
    grad_value = (back_signal.astype(jnp.float32) * key_proj.astype(jnp.float32)).astype(jnp.bfloat16)
    return (grad_query, grad_key, grad_value, taps_grad)
```

```python
import functools

import jax
import jax.numpy as jnp
import numpy as np
from jax import lax
from jax.experimental import pallas as pl
from jax.experimental.pallas import tpu as pltpu
from jax.sharding import PartitionSpec as P

MESH = pl.DeviceIdType.MESH
DEVICES = 256
INNER = 64
SIDE = 16
TOKENS = 128
CHANNELS = 1024
PARTS = 2
HELD = CHANNELS // DEVICES // PARTS
ROWS = 3 * HELD * DEVICES
SLAB = CHANNELS // PARTS
BF16 = jnp.bfloat16
F32 = jnp.float32


def make_tables():
    length = DEVICES * TOKENS
    outer = np.arange(DEVICES)
    inner = np.arange(TOKENS)
    theta = 2.0 * np.pi * (outer[:, None] + 0.25) * outer[None, :] / DEVICES
    first = np.concatenate([np.cos(theta), -np.sin(theta)], axis=0)
    last = first.T / length
    phase = 2.0 * np.pi * (outer[:, None] + 0.25) * inner[None, :] / length
    twist = np.concatenate([np.cos(phase), -np.sin(phase)], axis=1)
    turn = 2.0 * np.pi * ((inner[:, None] * inner[None, :]) % TOKENS) / TOKENS
    cosine, sine = np.cos(turn), np.sin(turn)
    there = np.block([[cosine, -sine], [sine, cosine]])
    back = np.block([[cosine, sine], [-sine, cosine]])
    return tuple(table.astype(np.float32) for table in (first, there, back, last, twist))


def where(device):
    return (device // INNER, device % INNER)


def at_offset(me, step):
    z = (me // 32 + step) % 8
    x = (me // 8 + step // 64) % 4
    y = (me // 2 + step // 16) % 4
    core = (me + step // 8) % 2
    return z * 32 + x * 8 + y * 2 + core


def one_dot(left, right):
    return jnp.dot(left, right, preferred_element_type=F32)


def halves(value):
    high = value.astype(BF16)
    return high, (value - high.astype(F32)).astype(BF16)


def kernel(
    query_hbm, key_hbm, value_hbm, taps_hbm, grad_hbm, first_hbm, there_hbm, back_hbm, last_hbm, twist_hbm,
    grad_query, grad_key, grad_value, grad_filter,
    query, key, value, taps, grad, first_wide, there_wide, back_wide, last_wide, twist, first, there, back, last,
    sent, landed, rows, result, returned, returned_in, load_sem, send_sem, recv_sem, return_sem, back_sem, cross_sem,
):
    me = lax.axis_index("dp") * INNER + lax.axis_index("ctx")
    barrier = pltpu.get_barrier_semaphore()
    group, member = me // SIDE, me % SIDE

    def along(step):
        return where(group * SIDE + (member + step) % SIDE)

    def across(step):
        return where(((group + step) % SIDE) * SIDE + member)

    @pl.loop(1, SIDE)
    def _(step):
        pl.semaphore_signal(barrier, inc=1, device_id=along(step), device_id_type=MESH)
        pl.semaphore_signal(barrier, inc=1, device_id=across(step), device_id_type=MESH)

    loads = []
    for place, (source, target) in enumerate((
        (key_hbm, key), (value_hbm, value), (grad_hbm, grad), (query_hbm, query), (taps_hbm, taps),
        (first_hbm, first_wide), (there_hbm, there_wide), (back_hbm, back_wide), (last_hbm, last_wide), (twist_hbm, twist),
    )):
        copy = pltpu.make_async_copy(source, target, load_sem.at[place])
        copy.start()
        loads.append(copy)
    for copy in loads[:5]:
        copy.wait()

    for part in range(PARTS):
        lines = pl.ds(part * SLAB, SLAB)
        source = key[lines].astype(F32) * value[lines].astype(F32)
        signal = grad[lines].astype(F32) * query[lines].astype(F32)
        sent[part, :, 0] = taps[lines].astype(F32).reshape(DEVICES, HELD, TOKENS).astype(BF16)
        sent[part, :, 1] = source.reshape(DEVICES, HELD, TOKENS).astype(BF16)
        sent[part, :, 2] = signal.reshape(DEVICES, HELD, TOKENS).astype(BF16)

    for copy in loads[5:]:
        copy.wait()
    for wide, table in ((first_wide, first), (there_wide, there), (back_wide, back), (last_wide, last)):
        table[0], table[1] = halves(wide[...])

    pl.semaphore_wait(barrier, 2 * (SIDE - 1))

    @pl.loop(1, SIDE)
    def _(step):
        pl.semaphore_signal(cross_sem, inc=1, device_id=across(step), device_id_type=MESH)

    pl.semaphore_wait(cross_sem, SIDE - 1)

    def scatter(outgoing, incoming, part, out_sem, in_sem):
        @pl.loop(1, DEVICES, unroll=5)
        def _(step):
            device = at_offset(me, step)
            pltpu.make_async_remote_copy(
                src_ref=outgoing.at[part, device],
                dst_ref=incoming.at[part, me],
                send_sem=out_sem.at[part],
                recv_sem=in_sem.at[part],
                device_id=where(device),
                device_id_type=MESH,
            ).start()

        pltpu.make_async_copy(outgoing.at[part, me], incoming.at[part, me], in_sem.at[part]).start()

    def all_in(incoming, part, in_sem):
        pltpu.make_async_copy(incoming.at[part], incoming.at[part], in_sem.at[part]).wait()

    def all_out(outgoing, part, out_sem):
        span = outgoing.at[part, pl.ds(0, DEVICES - 1)]
        pltpu.make_async_copy(span, span, out_sem.at[part]).wait()

    for part in range(PARTS):
        scatter(sent, landed, part, send_sem, recv_sem)

    def twisted(real, imag, sign):
        turn_real, turn_imag = twist[:, :TOKENS], sign * twist[:, TOKENS:]
        return real * turn_real - imag * turn_imag, real * turn_imag + imag * turn_real

    def triple(value, table):
        high, low = halves(value)
        return one_dot(high, table[0]) + (one_dot(low, table[0]) + one_dot(high, table[1]))

    @pl.loop(0, PARTS)
    def _(part):
        all_in(landed, part, recv_sem)
        rows[...] = landed[part].astype(F32).reshape(ROWS, TOKENS)
        columns = jnp.concatenate(
            [rows[pl.ds(line, DEVICES, stride=3 * HELD), :].astype(BF16) for line in range(3 * HELD)], axis=1
        )
        stage = one_dot(first[0], columns) + one_dot(first[1], columns)
        freq = []
        for line in range(3 * HELD):
            lanes = slice(line * TOKENS, (line + 1) * TOKENS)
            real, imag = twisted(stage[:DEVICES, lanes], stage[DEVICES:, lanes], 1.0)
            spectrum = triple(jnp.concatenate([real, imag], axis=1), there)
            freq.append((spectrum[:, :TOKENS], spectrum[:, TOKENS:]))
        pieces = []
        for which in range(3):
            for held in range(HELD):
                taps_freq, source_freq, signal_freq = (freq[array * HELD + held] for array in range(3))
                one, two = ((taps_freq, source_freq), (taps_freq, signal_freq), (source_freq, signal_freq))[which]
                if which == 0:
                    real = one[0] * two[0] - one[1] * two[1]
                    imag = one[0] * two[1] + one[1] * two[0]
                else:
                    real = one[0] * two[0] + one[1] * two[1]
                    imag = one[0] * two[1] - one[1] * two[0]
                spread = triple(jnp.concatenate([real, imag], axis=1), back)
                real, imag = twisted(spread[:, :TOKENS], spread[:, TOKENS:], -1.0)
                pieces.append(jnp.concatenate([real, imag], axis=0))
        high, low = halves(jnp.concatenate(pieces, axis=1))
        final = one_dot(last[0], high) + (one_dot(last[0], low) + one_dot(last[1], high))
        for line in range(3 * HELD):
            result[pl.ds(line, DEVICES, stride=3 * HELD), :] = final[:, line * TOKENS:(line + 1) * TOKENS]
        returned[part] = result[...].reshape(DEVICES, 3, HELD, TOKENS).astype(BF16)
        scatter(returned, returned_in, part, return_sem, back_sem)

    for part in range(PARTS):
        all_in(returned_in, part, back_sem)
        lines = pl.ds(part * SLAB, SLAB)
        convolved = returned_in[part, :, 0].astype(F32).reshape(SLAB, TOKENS)
        back_signal = returned_in[part, :, 1].astype(F32).reshape(SLAB, TOKENS)
        grad_query[lines] = (grad[lines].astype(F32) * convolved).astype(BF16)
        grad_key[lines] = (back_signal * value[lines].astype(F32)).astype(BF16)
        grad_value[lines] = (back_signal * key[lines].astype(F32)).astype(BF16)
        grad_filter[lines] = returned_in[part, :, 2].astype(F32).reshape(SLAB, TOKENS).astype(BF16)
    for part in range(PARTS):
        all_out(sent, part, send_sem)
        all_out(returned, part, return_sem)


def on_device(query_proj, key_proj, value_proj, filter_taps, grad_out):
    tables = make_tables()
    block = (CHANNELS, TOKENS)
    packed = (PARTS, DEVICES, 3, HELD, TOKENS)
    return pl.pallas_call(
        kernel,
        out_shape=[jax.ShapeDtypeStruct(block, BF16)] * 4,
        in_specs=[pl.BlockSpec(memory_space=pltpu.HBM)] * 10,
        out_specs=[pl.BlockSpec(memory_space=pltpu.VMEM)] * 4,
        scratch_shapes=[pltpu.VMEM(block, BF16)] * 5
        + [pltpu.VMEM(table.shape, F32) for table in tables]
        + [pltpu.VMEM((2,) + table.shape, BF16) for table in tables[:4]]
        + [
            pltpu.VMEM(packed, BF16),
            pltpu.VMEM(packed, BF16),
            pltpu.VMEM((ROWS, TOKENS), F32),
            pltpu.VMEM((ROWS, TOKENS), F32),
            pltpu.VMEM(packed, BF16),
            pltpu.VMEM(packed, BF16),
            pltpu.SemaphoreType.DMA((10,)),
            pltpu.SemaphoreType.DMA((PARTS,)),
            pltpu.SemaphoreType.DMA((PARTS,)),
            pltpu.SemaphoreType.DMA((PARTS,)),
            pltpu.SemaphoreType.DMA((PARTS,)),
            pltpu.SemaphoreType.REGULAR,
        ],
        compiler_params=pltpu.CompilerParams(
            collective_id=0, has_side_effects=True, vmem_limit_bytes=48 * 2**20
        ),
        name="gated_conv_backward",
    )(query_proj, key_proj, value_proj, filter_taps, grad_out, *(jnp.asarray(table) for table in tables))


def solution(mesh):
    spec = P(None, ("dp", "ctx"))
    return jax.shard_map(on_device, mesh=mesh, in_specs=(spec,) * 5, out_specs=(spec,) * 4, check_vma=False)
```

```python
import jax
import jax.numpy as jnp
import numpy as np
from jax import lax
from jax.experimental import pallas as pl
from jax.experimental.pallas import tpu as pltpu
from jax.sharding import PartitionSpec as P

LOGICAL = pl.DeviceIdType.LOGICAL
DEVICES = 256
INNER = 64
TOKENS = 128
CHANNELS = 1024
PARTS = 2
HELD = CHANNELS // DEVICES // PARTS
LINES = 3 * HELD
ROWS = LINES * DEVICES
SLAB = CHANNELS // PARTS
RING = (4, 3, 5, 2, 6, 1, 7, 0)
BF16 = jnp.bfloat16
F32 = jnp.float32


def make_tables():
    length = DEVICES * TOKENS
    outer = np.arange(DEVICES)
    inner = np.arange(TOKENS)
    theta = 2.0 * np.pi * (outer[:, None] + 0.25) * outer[None, :] / DEVICES
    cosine, sine = np.cos(theta), -np.sin(theta)
    phase = 2.0 * np.pi * (outer[:, None] + 0.25) * inner[None, :] / length
    twist = np.concatenate([np.cos(phase), -np.sin(phase)], axis=1)
    turn = 2.0 * np.pi * ((inner[:, None] * inner[None, :]) % TOKENS) / TOKENS
    there = np.block([[np.cos(turn), -np.sin(turn)], [np.sin(turn), np.cos(turn)]])
    back = np.block([[np.cos(turn), np.sin(turn)], [-np.sin(turn), np.cos(turn)]])
    stacked = [cosine, sine, there, back, cosine.T / length, sine.T / length, twist]
    return np.concatenate(stacked, axis=0).astype(np.float32)


def one_dot(left, right):
    return jnp.dot(left, right, preferred_element_type=F32)


def halves(value):
    high = value.astype(BF16)
    return high, (value - high.astype(F32)).astype(BF16)


def kernel(
    query_hbm, key_hbm, value_hbm, taps_hbm, grad_hbm, table_hbm, out,
    query, key, value, taps, grad, table, split, sent, landed, rows, result, returned, returned_in,
    load_sem, send_sem, recv_sem, return_sem, back_sem, cross_sem,
):
    me = lax.axis_index("dp") * INNER + lax.axis_index("ctx")
    low = lax.rem(me, 32)
    column = low // 8
    row = lax.rem(low // 2, 4)
    core = lax.rem(low, 2)
    ring = [lax.rem(me // 32 + step, 8) * 32 for step in range(8)]

    def beside(step_x, step_y, step_core):
        return lax.rem(column + step_x, 4) * 8 + lax.rem(row + step_y, 4) * 2 + lax.rem(core + step_core, 2)

    barrier = pltpu.get_barrier_semaphore()

    def greet(semaphore, device):
        pl.semaphore_signal(semaphore, inc=1, device_id=device, device_id_type=LOGICAL)

    for step in range(1, 4):
        greet(barrier, ring[0] + beside(0, step, 0))
    for step in RING[:7]:
        greet(barrier, ring[step] + low)

    @pl.loop(1, 8)
    def _(pair):
        place = beside(pair // 2, 0, lax.rem(pair, 2))
        for step in RING:
            greet(barrier, ring[step] + place)

    loads = []
    for place, (source, target) in enumerate((
        (key_hbm, key), (value_hbm, value), (grad_hbm, grad), (query_hbm, query), (taps_hbm, taps), (table_hbm, table),
    )):
        copy = pltpu.make_async_copy(source, target, load_sem.at[place])
        copy.start()
        loads.append(copy)
    for copy in loads[:5]:
        copy.wait()

    def pack(part):
        lines = pl.ds(part * SLAB, SLAB)
        shape = (DEVICES, HELD, TOKENS)
        sent[part, :, 0] = taps[lines].astype(F32).reshape(shape).astype(BF16)
        sent[part, :, 1] = (key[lines].astype(F32) * value[lines].astype(F32)).reshape(shape).astype(BF16)
        sent[part, :, 2] = (grad[lines].astype(F32) * query[lines].astype(F32)).reshape(shape).astype(BF16)

    def scatter(outgoing, incoming, part, out_sem, in_sem, wait=None):
        def send(device):
            pltpu.make_async_remote_copy(
                src_ref=outgoing.at[part, device],
                dst_ref=incoming.at[part, me],
                send_sem=out_sem.at[part],
                recv_sem=in_sem.at[part],
                device_id=device,
                device_id_type=LOGICAL,
            ).start()

        pltpu.make_async_copy(outgoing.at[part, me], incoming.at[part, me], in_sem.at[part]).start()
        for step in RING[:7]:
            send(ring[step] + low)

        def rest(step_y, first):
            @pl.loop(first, 8)
            def _(pair):
                place = beside(pair // 2, step_y, lax.rem(pair, 2))
                for step in RING:
                    send(ring[step] + place)

        for step_y in range(4):
            if wait is not None and step_y:
                wait(step_y)
            rest(step_y, 0 if step_y else 1)

    def all_in(incoming, part, in_sem):
        pltpu.make_async_copy(incoming.at[part], incoming.at[part], in_sem.at[part]).wait()

    def all_out(outgoing, part, out_sem):
        span = outgoing.at[part, pl.ds(0, DEVICES - 1)]
        pltpu.make_async_copy(span, span, out_sem.at[part]).wait()

    pack(0)
    pl.semaphore_wait(barrier, 66)
    for step in range(1, 4):
        greet(cross_sem.at[step], ring[0] + beside(0, step, 0))
    scatter(sent, landed, 0, send_sem, recv_sem, lambda step: pl.semaphore_wait(cross_sem.at[4 - step], 1))
    pack(1)
    scatter(sent, landed, 1, send_sem, recv_sem)

    loads[5].wait()
    split[0], split[1] = halves(table[pl.ds(0, 1536)])

    def twisted(real, imag, sign):
        turn_real, turn_imag = table[pl.ds(1536, DEVICES), :TOKENS], sign * table[pl.ds(1536, DEVICES), TOKENS:]
        return real * turn_real - imag * turn_imag, real * turn_imag + imag * turn_real

    def triple(value, lines):
        high, below = halves(value)
        return one_dot(high, split[0, lines]) + (one_dot(below, split[0, lines]) + one_dot(high, split[1, lines]))

    @pl.loop(0, PARTS)
    def _(part):
        all_in(landed, part, recv_sem)
        rows[...] = landed[part].astype(F32).reshape(ROWS, TOKENS)
        columns = jnp.concatenate(
            [rows[pl.ds(line, DEVICES, stride=LINES), :].astype(BF16) for line in range(LINES)], axis=1
        )
        stage = one_dot(split[0, 0:512], columns) + one_dot(split[1, 0:512], columns)
        freq = []
        for line in range(LINES):
            lanes = slice(line * TOKENS, (line + 1) * TOKENS)
            real, imag = twisted(stage[:DEVICES, lanes], stage[DEVICES:, lanes], 1.0)
            spectrum = triple(jnp.concatenate([real, imag], axis=1), slice(512, 768))
            freq.append((spectrum[:, :TOKENS], spectrum[:, TOKENS:]))
        pieces = []
        for which in range(3):
            for held in range(HELD):
                taps_freq, source_freq, signal_freq = (freq[array * HELD + held] for array in range(3))
                one, two = ((taps_freq, source_freq), (taps_freq, signal_freq), (source_freq, signal_freq))[which]
                if which == 0:
                    real = one[0] * two[0] - one[1] * two[1]
                    imag = one[0] * two[1] + one[1] * two[0]
                else:
                    real = one[0] * two[0] + one[1] * two[1]
                    imag = one[0] * two[1] - one[1] * two[0]
                spread = triple(jnp.concatenate([real, imag], axis=1), slice(768, 1024))
                pieces.append(twisted(spread[:, :TOKENS], spread[:, TOKENS:], -1.0))
        final = 0.0
        for side in range(2):
            high, below = halves(jnp.concatenate([piece[side] for piece in pieces], axis=1))
            lines = slice(1024 + side * DEVICES, 1280 + side * DEVICES)
            final += one_dot(split[0, lines], high) + (one_dot(split[0, lines], below) + one_dot(split[1, lines], high))
        for line in range(LINES):
            result[pl.ds(line, DEVICES, stride=LINES), :] = final[:, line * TOKENS:(line + 1) * TOKENS]
        returned[part] = result[...].reshape(DEVICES, 3, HELD, TOKENS).astype(BF16)
        scatter(returned, returned_in, part, return_sem, back_sem)

    for part in range(PARTS):
        all_in(returned_in, part, back_sem)
        for which in range(3):
            out[which, pl.ds(part * SLAB, SLAB)] = returned_in[part, :, which].astype(F32).reshape(SLAB, TOKENS).astype(BF16)
    for part in range(PARTS):
        all_out(sent, part, send_sem)
        all_out(returned, part, return_sem)


def gate(back, key, value, grad, grad_query, grad_key, grad_value, grad_filter):
    back_signal = back[1].astype(F32)
    grad_query[...] = (grad[...].astype(F32) * back[0].astype(F32)).astype(BF16)
    grad_key[...] = (back_signal * value[...].astype(F32)).astype(BF16)
    grad_value[...] = (back_signal * key[...].astype(F32)).astype(BF16)
    grad_filter[...] = back[2]


def on_device(query_proj, key_proj, value_proj, filter_taps, grad_out):
    table = make_tables()
    block = (CHANNELS, TOKENS)
    packed = (PARTS, DEVICES, 3, HELD, TOKENS)
    back = pl.pallas_call(
        kernel,
        out_shape=jax.ShapeDtypeStruct((3,) + block, BF16),
        in_specs=[pl.BlockSpec(memory_space=pltpu.HBM)] * 6,
        out_specs=pl.BlockSpec(memory_space=pltpu.VMEM),
        scratch_shapes=[pltpu.VMEM(block, BF16)] * 5
        + [
            pltpu.VMEM(table.shape, F32),
            pltpu.VMEM((2, 1536, DEVICES), BF16),
            pltpu.VMEM(packed, BF16),
            pltpu.VMEM(packed, BF16),
            pltpu.VMEM((ROWS, TOKENS), F32),
            pltpu.VMEM((ROWS, TOKENS), F32),
            pltpu.VMEM(packed, BF16),
            pltpu.VMEM(packed, BF16),
            pltpu.SemaphoreType.DMA((6,)),
            pltpu.SemaphoreType.DMA((PARTS,)),
            pltpu.SemaphoreType.DMA((PARTS,)),
            pltpu.SemaphoreType.DMA((PARTS,)),
            pltpu.SemaphoreType.DMA((PARTS,)),
            pltpu.SemaphoreType.REGULAR((4,)),
        ],
        compiler_params=pltpu.CompilerParams(
            collective_id=0, has_side_effects=True, vmem_limit_bytes=63 * 2**20
        ),
        name="transform_and_exchange",
    )(query_proj, key_proj, value_proj, filter_taps, grad_out, jnp.asarray(table))
    return pl.pallas_call(
        gate,
        grid=(2,),
        out_shape=[jax.ShapeDtypeStruct(block, BF16)] * 4,
        in_specs=[pl.BlockSpec((3, CHANNELS // 2, TOKENS), lambda i: (0, i, 0))]
        + [pl.BlockSpec((CHANNELS // 2, TOKENS), lambda i: (i, 0))] * 3,
        out_specs=[pl.BlockSpec((CHANNELS // 2, TOKENS), lambda i: (i, 0))] * 4,
        name="gate_results",
    )(back, key_proj, value_proj, grad_out)


def solution(mesh):
    spec = P(None, ("dp", "ctx"))
    return jax.shard_map(on_device, mesh=mesh, in_specs=(spec,) * 5, out_specs=(spec,) * 4, check_vma=False)
```

```python
import jax
import jax.numpy as jnp
import numpy as np
from jax import lax
from jax.experimental import pallas as pl
from jax.experimental.pallas import tpu as pltpu
from jax.sharding import PartitionSpec as P

LOGICAL = pl.DeviceIdType.LOGICAL
DEVICES = 256
INNER = 64
TOKENS = 128
CHANNELS = 1024
PARTS = 2
HELD = CHANNELS // DEVICES // PARTS
LINES = 3 * HELD
ROWS = LINES * DEVICES
SLAB = CHANNELS // PARTS
RING = (4, 3, 5, 2, 6, 1, 7, 0)
BF16 = jnp.bfloat16
F32 = jnp.float32


def make_tables():
    length = DEVICES * TOKENS
    outer = np.arange(DEVICES)
    inner = np.arange(TOKENS)
    theta = 2.0 * np.pi * (outer[:, None] + 0.25) * outer[None, :] / DEVICES
    cosine, sine = np.cos(theta), -np.sin(theta)
    phase = 2.0 * np.pi * (outer[:, None] + 0.25) * inner[None, :] / length
    twist = np.concatenate([np.cos(phase), -np.sin(phase)], axis=1)
    turn = 2.0 * np.pi * ((inner[:, None] * inner[None, :]) % TOKENS) / TOKENS
    there = np.block([[np.cos(turn), -np.sin(turn)], [np.sin(turn), np.cos(turn)]])
    back = np.block([[np.cos(turn), np.sin(turn)], [-np.sin(turn), np.cos(turn)]])
    stacked = [cosine, sine, there, back, cosine.T / length, sine.T / length, twist]
    return np.concatenate(stacked, axis=0).astype(np.float32)


def one_dot(left, right):
    return jnp.dot(left, right, preferred_element_type=F32)


def halves(value):
    high = value.astype(BF16)
    return high, (value - high.astype(F32)).astype(BF16)


def kernel(
    query_hbm, key_hbm, value_hbm, taps_hbm, grad_hbm, table_hbm, out,
    query, key, value, taps, grad, table, split, sent, landed, rows, result, returned, returned_in,
    load_sem, send_sem, recv_sem, return_sem, back_sem, cross_sem,
):
    me = lax.axis_index("dp") * INNER + lax.axis_index("ctx")
    low = lax.rem(me, 32)
    column = low // 8
    row = lax.rem(low // 2, 4)
    core = lax.rem(low, 2)
    ring = [lax.rem(me // 32 + step, 8) * 32 for step in range(8)]

    def beside(step_x, step_y, step_core):
        return lax.rem(column + step_x, 4) * 8 + lax.rem(row + step_y, 4) * 2 + lax.rem(core + step_core, 2)

    barrier = pltpu.get_barrier_semaphore()

    def greet(semaphore, device):
        pl.semaphore_signal(semaphore, inc=1, device_id=device, device_id_type=LOGICAL)

    for step in range(1, 4):
        greet(barrier, ring[0] + beside(step, 0, 0))
        greet(barrier, ring[0] + beside(0, step, 0))
    twin = beside(0, 0, 1)
    for step in RING:
        if step:
            greet(barrier, ring[step] + low)
        greet(barrier, ring[step] + twin)

    loads = []
    for part in range(PARTS):
        lines = pl.ds(part * SLAB, SLAB)
        group = []
        for place, (source, target) in enumerate((
            (taps_hbm, taps), (key_hbm, key), (value_hbm, value), (grad_hbm, grad), (query_hbm, query),
        )):
            copy = pltpu.make_async_copy(source.at[lines], target.at[lines], load_sem.at[part, place])
            copy.start()
            group.append(copy)
        loads.append(group)
    table_load = pltpu.make_async_copy(table_hbm, table, load_sem.at[0, 5])
    table_load.start()

    def pack(part):
        for copy in loads[part]:
            copy.wait()
        lines = pl.ds(part * SLAB, SLAB)
        shape = (DEVICES, HELD, TOKENS)
        sent[part, :, 0] = taps[lines].astype(F32).reshape(shape).astype(BF16)
        sent[part, :, 1] = (key[lines].astype(F32) * value[lines].astype(F32)).reshape(shape).astype(BF16)
        sent[part, :, 2] = (grad[lines].astype(F32) * query[lines].astype(F32)).reshape(shape).astype(BF16)

    def scatter(outgoing, incoming, part, out_sem, in_sem, wait_x=None, wait_y=None):
        def send(device):
            pltpu.make_async_remote_copy(
                src_ref=outgoing.at[part, device],
                dst_ref=incoming.at[part, me],
                send_sem=out_sem.at[part],
                recv_sem=in_sem.at[part],
                device_id=device,
                device_id_type=LOGICAL,
            ).start()

        pltpu.make_async_copy(outgoing.at[part, me], incoming.at[part, me], in_sem.at[part]).start()
        for step in RING[:7]:
            send(ring[step] + low)

        def line(step_x, step_y):
            for step_core in range(2):
                place = beside(step_x, step_y, step_core)
                for step in RING:
                    send(ring[step] + place)

        for step in RING:
            send(ring[step] + twin)
        if wait_x is not None:
            wait_x()

        @pl.loop(1, 4)
        def _(step_x):
            line(step_x, 0)

        for step_y in range(1, 4):
            if wait_y is not None:
                wait_y(step_y)

            @pl.loop(0, 4)
            def _(step_x):
                line(step_x, step_y)

    def all_in(incoming, part, in_sem):
        pltpu.make_async_copy(incoming.at[part], incoming.at[part], in_sem.at[part]).wait()

    def all_out(outgoing, part, out_sem):
        span = outgoing.at[part, pl.ds(0, DEVICES - 1)]
        pltpu.make_async_copy(span, span, out_sem.at[part]).wait()

    pack(0)
    pl.semaphore_wait(barrier, 21)
    for step in range(1, 4):
        greet(cross_sem.at[0, step], ring[0] + beside(step, 0, 0))

    def plane_in():
        for step in range(1, 4):
            pl.semaphore_wait(cross_sem.at[0, 4 - step], 1)
        for step in range(1, 4):
            greet(cross_sem.at[1, step], ring[0] + beside(0, step, 0))

    def other_in(step):
        pl.semaphore_wait(cross_sem.at[1, 4 - step], 1)

    scatter(sent, landed, 0, send_sem, recv_sem, plane_in, other_in)
    pack(1)
    scatter(sent, landed, 1, send_sem, recv_sem)

    table_load.wait()
    split[0], split[1] = halves(table[pl.ds(0, 1536)])

    def twisted(real, imag, sign):
        turn_real, turn_imag = table[pl.ds(1536, DEVICES), :TOKENS], sign * table[pl.ds(1536, DEVICES), TOKENS:]
        return real * turn_real - imag * turn_imag, real * turn_imag + imag * turn_real

    def triple(value, lines):
        high, below = halves(value)
        return one_dot(high, split[0, lines]) + (one_dot(below, split[0, lines]) + one_dot(high, split[1, lines]))

    @pl.loop(0, PARTS)
    def _(part):
        all_in(landed, part, recv_sem)
        rows[...] = landed[part].astype(F32).reshape(ROWS, TOKENS)
        columns = jnp.concatenate(
            [rows[pl.ds(line, DEVICES, stride=LINES), :].astype(BF16) for line in range(LINES)], axis=1
        )
        stage = one_dot(split[0, 0:512], columns) + one_dot(split[1, 0:512], columns)
        freq = []
        for line in range(LINES):
            lanes = slice(line * TOKENS, (line + 1) * TOKENS)
            real, imag = twisted(stage[:DEVICES, lanes], stage[DEVICES:, lanes], 1.0)
            spectrum = triple(jnp.concatenate([real, imag], axis=1), slice(512, 768))
            freq.append((spectrum[:, :TOKENS], spectrum[:, TOKENS:]))
        pieces = []
        for which in range(3):
            for held in range(HELD):
                taps_freq, source_freq, signal_freq = (freq[array * HELD + held] for array in range(3))
                one, two = ((taps_freq, source_freq), (taps_freq, signal_freq), (source_freq, signal_freq))[which]
                if which == 0:
                    real = one[0] * two[0] - one[1] * two[1]
                    imag = one[0] * two[1] + one[1] * two[0]
                else:
                    real = one[0] * two[0] + one[1] * two[1]
                    imag = one[0] * two[1] - one[1] * two[0]
                spread = triple(jnp.concatenate([real, imag], axis=1), slice(768, 1024))
                pieces.append(twisted(spread[:, :TOKENS], spread[:, TOKENS:], -1.0))
        final = 0.0
        for side in range(2):
            high, below = halves(jnp.concatenate([piece[side] for piece in pieces], axis=1))
            lines = slice(1024 + side * DEVICES, 1280 + side * DEVICES)
            final += one_dot(split[0, lines], high) + (one_dot(split[0, lines], below) + one_dot(split[1, lines], high))
        for line in range(LINES):
            result[pl.ds(line, DEVICES, stride=LINES), :] = final[:, line * TOKENS:(line + 1) * TOKENS]
        returned[part] = result[...].reshape(DEVICES, 3, HELD, TOKENS).astype(BF16)
        scatter(returned, returned_in, part, return_sem, back_sem)

    for part in range(PARTS):
        all_in(returned_in, part, back_sem)
        lines = pl.ds(part * SLAB, SLAB)
        convolved, back_signal, taps_grad = (
            returned_in[part, :, which].astype(F32).reshape(SLAB, TOKENS) for which in range(3)
        )
        out[0, lines] = (grad[lines].astype(F32) * convolved).astype(BF16)
        out[1, lines] = (back_signal * value[lines].astype(F32)).astype(BF16)
        out[2, lines] = (back_signal * key[lines].astype(F32)).astype(BF16)
        out[3, lines] = taps_grad.astype(BF16)
    for part in range(PARTS):
        all_out(sent, part, send_sem)
        all_out(returned, part, return_sem)


def deal(stacked, grad_query, grad_key, grad_value, grad_filter, sems):
    copies = [
        pltpu.make_async_copy(stacked.at[place], target, sems.at[place])
        for place, target in enumerate((grad_query, grad_key, grad_value, grad_filter))
    ]
    for copy in copies:
        copy.start()
    for copy in copies:
        copy.wait()


def on_device(query_proj, key_proj, value_proj, filter_taps, grad_out):
    table = make_tables()
    block = (CHANNELS, TOKENS)
    packed = (PARTS, DEVICES, 3, HELD, TOKENS)
    operands = [
        pltpu.with_memory_space_constraint(operand, pltpu.HBM)
        for operand in (query_proj, key_proj, value_proj, filter_taps, grad_out, jnp.asarray(table))
    ]
    stacked = pl.pallas_call(
        kernel,
        out_shape=pltpu.VMEM((4,) + block, BF16),
        in_specs=[pl.BlockSpec(memory_space=pltpu.HBM)] * 6,
        out_specs=pl.BlockSpec(memory_space=pltpu.VMEM),
        scratch_shapes=[pltpu.VMEM(block, BF16)] * 5
        + [
            pltpu.VMEM(table.shape, F32),
            pltpu.VMEM((2, 1536, DEVICES), BF16),
            pltpu.VMEM(packed, BF16),
            pltpu.VMEM(packed, BF16),
            pltpu.VMEM((ROWS, TOKENS), F32),
            pltpu.VMEM((ROWS, TOKENS), F32),
            pltpu.VMEM(packed, BF16),
            pltpu.VMEM(packed, BF16),
            pltpu.SemaphoreType.DMA((PARTS, 6)),
            pltpu.SemaphoreType.DMA((PARTS,)),
            pltpu.SemaphoreType.DMA((PARTS,)),
            pltpu.SemaphoreType.DMA((PARTS,)),
            pltpu.SemaphoreType.DMA((PARTS,)),
            pltpu.SemaphoreType.REGULAR((2, 4)),
        ],
        compiler_params=pltpu.CompilerParams(
            collective_id=0, has_side_effects=True, vmem_limit_bytes=40 * 2**20
        ),
        name="transform_and_exchange",
    )(*operands)
    return pl.pallas_call(
        deal,
        out_shape=[jax.ShapeDtypeStruct(block, BF16)] * 4,
        in_specs=[pl.BlockSpec(memory_space=pltpu.VMEM)],
        out_specs=[pl.BlockSpec(memory_space=pltpu.HBM)] * 4,
        scratch_shapes=[pltpu.SemaphoreType.DMA((4,))],
        name="gate_results",
    )(pltpu.with_memory_space_constraint(stacked, pltpu.VMEM))


def solution(mesh):
    spec = P(None, ("dp", "ctx"))
    return jax.shard_map(on_device, mesh=mesh, in_specs=(spec,) * 5, out_specs=(spec,) * 4, check_vma=False)
```

```python
import jax
import jax.numpy as jnp
import numpy as np
from jax import lax
from jax.experimental import pallas as pl
from jax.experimental.pallas import tpu as pltpu
from jax.sharding import PartitionSpec as P

LOGICAL = pl.DeviceIdType.LOGICAL
DEVICES = 256
INNER = 64
TOKENS = 128
CHANNELS = 1024
PARTS = 2
HELD = CHANNELS // DEVICES // PARTS
LINES = 3 * HELD
ROWS = LINES * DEVICES
SLAB = CHANNELS // PARTS
RING = (4, 3, 5, 2, 6, 1, 7, 0)
BF16 = jnp.bfloat16
F32 = jnp.float32


def make_tables():
    length = DEVICES * TOKENS
    outer = np.arange(DEVICES)
    inner = np.arange(TOKENS)
    theta = 2.0 * np.pi * (outer[:, None] + 0.25) * outer[None, :] / DEVICES
    cosine, sine = np.cos(theta), -np.sin(theta)
    phase = 2.0 * np.pi * (outer[:, None] + 0.25) * inner[None, :] / length
    twist = np.concatenate([np.cos(phase), -np.sin(phase)], axis=1)
    turn = 2.0 * np.pi * ((inner[:, None] * inner[None, :]) % TOKENS) / TOKENS
    there = np.block([[np.cos(turn), -np.sin(turn)], [np.sin(turn), np.cos(turn)]])
    back = np.block([[np.cos(turn), np.sin(turn)], [-np.sin(turn), np.cos(turn)]])
    stacked = [cosine, sine, there, back, cosine.T / length, sine.T / length, twist]
    return np.concatenate(stacked, axis=0).astype(np.float32)


def one_dot(left, right):
    return jnp.dot(left, right, preferred_element_type=F32)


def halves(value):
    high = value.astype(BF16)
    return high, (value - high.astype(F32)).astype(BF16)


def kernel(
    query_hbm, key_hbm, value_hbm, taps_hbm, grad_hbm, table_hbm, out,
    query, key, value, taps, grad, table, split, sent, landed, rows, result, returned, returned_in,
    load_sem, send_sem, recv_sem, return_sem, back_sem, cross_sem,
):
    me = lax.axis_index("dp") * INNER + lax.axis_index("ctx")
    low = lax.rem(me, 32)
    column = low // 8
    row = lax.rem(low // 2, 4)
    core = lax.rem(low, 2)
    ring = [lax.rem(me // 32 + step, 8) * 32 for step in range(8)]

    def beside(step_x, step_y, step_core):
        return lax.rem(column + step_x, 4) * 8 + lax.rem(row + step_y, 4) * 2 + lax.rem(core + step_core, 2)

    barrier = pltpu.get_barrier_semaphore()

    def greet(semaphore, device):
        pl.semaphore_signal(semaphore, inc=1, device_id=device, device_id_type=LOGICAL)

    twin = beside(0, 0, 1)
    for step in RING:
        if step:
            greet(barrier, ring[step] + low)
        greet(barrier, ring[step] + twin)

    @pl.loop(1, 16, unroll=5)
    def _(line):
        greet(barrier, ring[0] + beside(line // 4, lax.rem(line, 4), 0))

    loads = []
    for part in range(PARTS):
        lines = pl.ds(part * SLAB, SLAB)
        group = []
        for place, (source, target) in enumerate((
            (taps_hbm, taps), (key_hbm, key), (value_hbm, value), (grad_hbm, grad), (query_hbm, query),
        )):
            copy = pltpu.make_async_copy(source.at[lines], target.at[lines], load_sem.at[part, place])
            copy.start()
            group.append(copy)
        loads.append(group)
    table_load = pltpu.make_async_copy(table_hbm, table, load_sem.at[0, 5])
    table_load.start()

    def pack(part):
        for copy in loads[part]:
            copy.wait()
        lines = pl.ds(part * SLAB, SLAB)
        shape = (DEVICES, HELD, TOKENS)
        sent[part, :, 0] = taps[lines].astype(F32).reshape(shape).astype(BF16)
        sent[part, :, 1] = (key[lines].astype(F32) * value[lines].astype(F32)).reshape(shape).astype(BF16)
        sent[part, :, 2] = (grad[lines].astype(F32) * query[lines].astype(F32)).reshape(shape).astype(BF16)

    def send(outgoing, incoming, part, out_sem, in_sem, device):
        pltpu.make_async_remote_copy(
            src_ref=outgoing.at[part, device],
            dst_ref=incoming.at[part, me],
            send_sem=out_sem.at[part],
            recv_sem=in_sem.at[part],
            device_id=device,
            device_id_type=LOGICAL,
        ).start()

    def send_own_line(*route):
        outgoing, incoming, part, _, in_sem = route
        pltpu.make_async_copy(outgoing.at[part, me], incoming.at[part, me], in_sem.at[part]).start()
        for step in RING:
            if step:
                send(*route, ring[step] + low)
            send(*route, ring[step] + twin)

    def send_lines(*route, ready=None):
        @pl.loop(1, 16)
        def _(line):
            step_x, step_y = line // 4, lax.rem(line, 4)
            if ready is not None:
                ready(lax.rem(4 - step_x, 4) * 4 + lax.rem(4 - step_y, 4))
            for step_core in range(2):
                place = beside(step_x, step_y, step_core)
                for step in RING:
                    send(*route, ring[step] + place)

    def all_in(incoming, part, in_sem):
        pltpu.make_async_copy(incoming.at[part], incoming.at[part], in_sem.at[part]).wait()

    def all_out(outgoing, part, out_sem):
        span = outgoing.at[part, pl.ds(0, DEVICES - 1)]
        pltpu.make_async_copy(span, span, out_sem.at[part]).wait()

    pack(0)
    pack(1)
    pl.semaphore_wait(barrier, 30)

    @pl.loop(1, 16, unroll=5)
    def _(line):
        greet(cross_sem.at[line], ring[0] + beside(line // 4, lax.rem(line, 4), 0))

    for part in range(PARTS):
        send_own_line(sent, landed, part, send_sem, recv_sem)
    send_lines(sent, landed, 0, send_sem, recv_sem, ready=lambda line: pl.semaphore_wait(cross_sem.at[line], 1))
    send_lines(sent, landed, 1, send_sem, recv_sem)

    table_load.wait()
    split[0], split[1] = halves(table[pl.ds(0, 1536)])

    def twisted(real, imag, sign):
        turn_real, turn_imag = table[pl.ds(1536, DEVICES), :TOKENS], sign * table[pl.ds(1536, DEVICES), TOKENS:]
        return real * turn_real - imag * turn_imag, real * turn_imag + imag * turn_real

    def triple(value, lines):
        high, below = halves(value)
        return one_dot(high, split[0, lines]) + (one_dot(below, split[0, lines]) + one_dot(high, split[1, lines]))

    @pl.loop(0, PARTS)
    def _(part):
        all_in(landed, part, recv_sem)
        rows[...] = landed[part].astype(F32).reshape(ROWS, TOKENS)
        columns = jnp.concatenate(
            [rows[pl.ds(line, DEVICES, stride=LINES), :].astype(BF16) for line in range(LINES)], axis=1
        )
        stage = one_dot(split[0, 0:512], columns) + one_dot(split[1, 0:512], columns)
        freq = []
        for line in range(LINES):
            lanes = slice(line * TOKENS, (line + 1) * TOKENS)
            real, imag = twisted(stage[:DEVICES, lanes], stage[DEVICES:, lanes], 1.0)
            spectrum = triple(jnp.concatenate([real, imag], axis=1), slice(512, 768))
            freq.append((spectrum[:, :TOKENS], spectrum[:, TOKENS:]))
        pieces = []
        for which in range(3):
            for held in range(HELD):
                taps_freq, source_freq, signal_freq = (freq[array * HELD + held] for array in range(3))
                one, two = ((taps_freq, source_freq), (taps_freq, signal_freq), (source_freq, signal_freq))[which]
                if which == 0:
                    real = one[0] * two[0] - one[1] * two[1]
                    imag = one[0] * two[1] + one[1] * two[0]
                else:
                    real = one[0] * two[0] + one[1] * two[1]
                    imag = one[0] * two[1] - one[1] * two[0]
                spread = triple(jnp.concatenate([real, imag], axis=1), slice(768, 1024))
                pieces.append(twisted(spread[:, :TOKENS], spread[:, TOKENS:], -1.0))
        final = 0.0
        for side in range(2):
            high, below = halves(jnp.concatenate([piece[side] for piece in pieces], axis=1))
            lines = slice(1024 + side * DEVICES, 1280 + side * DEVICES)
            final += one_dot(split[0, lines], high) + (one_dot(split[0, lines], below) + one_dot(split[1, lines], high))
        for line in range(LINES):
            result[pl.ds(line, DEVICES, stride=LINES), :] = final[:, line * TOKENS:(line + 1) * TOKENS]
        returned[part] = result[...].reshape(DEVICES, 3, HELD, TOKENS).astype(BF16)
        send_own_line(returned, returned_in, part, return_sem, back_sem)
        send_lines(returned, returned_in, part, return_sem, back_sem)

    for part in range(PARTS):
        all_in(returned_in, part, back_sem)
        lines = pl.ds(part * SLAB, SLAB)
        convolved, back_signal, taps_grad = (
            returned_in[part, :, which].astype(F32).reshape(SLAB, TOKENS) for which in range(3)
        )
        out[0, lines] = (grad[lines].astype(F32) * convolved).astype(BF16)
        out[1, lines] = (back_signal * value[lines].astype(F32)).astype(BF16)
        out[2, lines] = (back_signal * key[lines].astype(F32)).astype(BF16)
        out[3, lines] = taps_grad.astype(BF16)
    for part in range(PARTS):
        all_out(sent, part, send_sem)
        all_out(returned, part, return_sem)


def deal(stacked, grad_query, grad_key, grad_value, grad_filter, sems):
    copies = [
        pltpu.make_async_copy(stacked.at[place], target, sems.at[place])
        for place, target in enumerate((grad_query, grad_key, grad_value, grad_filter))
    ]
    for copy in copies:
        copy.start()
    for copy in copies:
        copy.wait()


def on_device(query_proj, key_proj, value_proj, filter_taps, grad_out):
    table = make_tables()
    block = (CHANNELS, TOKENS)
    packed = (PARTS, DEVICES, 3, HELD, TOKENS)
    operands = [
        pltpu.with_memory_space_constraint(operand, pltpu.HBM)
        for operand in (query_proj, key_proj, value_proj, filter_taps, grad_out, jnp.asarray(table))
    ]
    stacked = pl.pallas_call(
        kernel,
        out_shape=pltpu.VMEM((4,) + block, BF16),
        in_specs=[pl.BlockSpec(memory_space=pltpu.HBM)] * 6,
        out_specs=pl.BlockSpec(memory_space=pltpu.VMEM),
        scratch_shapes=[pltpu.VMEM(block, BF16)] * 5
        + [
            pltpu.VMEM(table.shape, F32),
            pltpu.VMEM((2, 1536, DEVICES), BF16),
            pltpu.VMEM(packed, BF16),
            pltpu.VMEM(packed, BF16),
            pltpu.VMEM((ROWS, TOKENS), F32),
            pltpu.VMEM((ROWS, TOKENS), F32),
            pltpu.VMEM(packed, BF16),
            pltpu.VMEM(packed, BF16),
            pltpu.SemaphoreType.DMA((PARTS, 6)),
            pltpu.SemaphoreType.DMA((PARTS,)),
            pltpu.SemaphoreType.DMA((PARTS,)),
            pltpu.SemaphoreType.DMA((PARTS,)),
            pltpu.SemaphoreType.DMA((PARTS,)),
            pltpu.SemaphoreType.REGULAR((16,)),
        ],
        compiler_params=pltpu.CompilerParams(
            collective_id=0, has_side_effects=True, vmem_limit_bytes=40 * 2**20
        ),
        name="transform_and_exchange",
    )(*operands)
    return pl.pallas_call(
        deal,
        out_shape=[jax.ShapeDtypeStruct(block, BF16)] * 4,
        in_specs=[pl.BlockSpec(memory_space=pltpu.VMEM)],
        out_specs=[pl.BlockSpec(memory_space=pltpu.HBM)] * 4,
        scratch_shapes=[pltpu.SemaphoreType.DMA((4,))],
        name="gate_results",
    )(pltpu.with_memory_space_constraint(stacked, pltpu.VMEM))


def solution(mesh):
    spec = P(None, ("dp", "ctx"))
    return jax.shard_map(on_device, mesh=mesh, in_specs=(spec,) * 5, out_specs=(spec,) * 4, check_vma=False)
```

```python
import jax
import jax.numpy as jnp
import numpy as np
from jax import lax
from jax.experimental import pallas as pl
from jax.experimental.pallas import tpu as pltpu
from jax.sharding import PartitionSpec as P

LOGICAL = pl.DeviceIdType.LOGICAL
DEVICES = 256
INNER = 64
TOKENS = 128
CHANNELS = 1024
PARTS = 2
HELD = CHANNELS // DEVICES // PARTS
LINES = 3 * HELD
ROWS = LINES * DEVICES
SLAB = CHANNELS // PARTS
RING = (4, 3, 5, 2, 6, 1, 7, 0)
BF16 = jnp.bfloat16
F32 = jnp.float32


def make_tables():
    length = DEVICES * TOKENS
    outer = np.arange(DEVICES)
    inner = np.arange(TOKENS)
    theta = 2.0 * np.pi * (outer[:, None] + 0.25) * outer[None, :] / DEVICES
    cosine, sine = np.cos(theta), -np.sin(theta)
    phase = 2.0 * np.pi * (outer[:, None] + 0.25) * inner[None, :] / length
    twist = np.concatenate([np.cos(phase), -np.sin(phase)], axis=1)
    turn = 2.0 * np.pi * ((inner[:, None] * inner[None, :]) % TOKENS) / TOKENS
    there = np.block([[np.cos(turn), -np.sin(turn)], [np.sin(turn), np.cos(turn)]])
    back = np.block([[np.cos(turn), np.sin(turn)], [-np.sin(turn), np.cos(turn)]])
    stacked = [cosine, sine, there, back, cosine.T / length, sine.T / length, twist]
    return np.concatenate(stacked, axis=0).astype(np.float32)


def one_dot(left, right):
    return jnp.dot(left, right, preferred_element_type=F32)


def halves(value):
    high = value.astype(BF16)
    return high, (value - high.astype(F32)).astype(BF16)


def kernel(
    query_hbm, key_hbm, value_hbm, taps_hbm, grad_hbm, table_hbm, out,
    query, key, value, taps, grad, table, split, sent, landed, rows, result, returned, returned_in,
    load_sem, send_sem, recv_sem, return_sem, back_sem, cross_sem,
):
    me = lax.axis_index("dp") * INNER + lax.axis_index("ctx")
    low = lax.rem(me, 32)
    column = low // 8
    row = lax.rem(low // 2, 4)
    core = lax.rem(low, 2)
    ring = [lax.rem(me // 32 + step, 8) * 32 for step in range(8)]

    def beside(step_x, step_y, step_core):
        return lax.rem(column + step_x, 4) * 8 + lax.rem(row + step_y, 4) * 2 + lax.rem(core + step_core, 2)

    loads = []
    for part in range(PARTS):
        lines = pl.ds(part * SLAB, SLAB)
        group = []
        for place, (source, target) in enumerate((
            (taps_hbm, taps), (key_hbm, key), (value_hbm, value), (grad_hbm, grad), (query_hbm, query),
        )):
            copy = pltpu.make_async_copy(source.at[lines], target.at[lines], load_sem.at[part, place])
            copy.start()
            group.append(copy)
        loads.append(group)
    barrier = pltpu.get_barrier_semaphore()

    def greet(semaphore, device):
        pl.semaphore_signal(semaphore, inc=1, device_id=device, device_id_type=LOGICAL)

    twin = beside(0, 0, 1)
    for step in RING:
        if step:
            greet(barrier, ring[step] + low)
        greet(barrier, ring[step] + twin)

    @pl.loop(1, 16, unroll=5)
    def _(line):
        greet(barrier, ring[0] + beside(line // 4, lax.rem(line, 4), 0))

    table_load = pltpu.make_async_copy(table_hbm, table, load_sem.at[0, 5])
    table_load.start()

    def pack(part):
        for copy in loads[part]:
            copy.wait()
        lines = pl.ds(part * SLAB, SLAB)
        shape = (DEVICES, HELD, TOKENS)
        sent[part, :, 0] = taps[lines].astype(F32).reshape(shape).astype(BF16)
        sent[part, :, 1] = (key[lines].astype(F32) * value[lines].astype(F32)).reshape(shape).astype(BF16)
        sent[part, :, 2] = (grad[lines].astype(F32) * query[lines].astype(F32)).reshape(shape).astype(BF16)

    def send(outgoing, incoming, part, out_sem, in_sem, device):
        pltpu.make_async_remote_copy(
            src_ref=outgoing.at[part, device],
            dst_ref=incoming.at[part, me],
            send_sem=out_sem.at[part],
            recv_sem=in_sem.at[part],
            device_id=device,
            device_id_type=LOGICAL,
        ).start()

    def send_own_line(*route):
        outgoing, incoming, part, _, in_sem = route
        pltpu.make_async_copy(outgoing.at[part, me], incoming.at[part, me], in_sem.at[part]).start()
        for step in RING:
            if step:
                send(*route, ring[step] + low)
            send(*route, ring[step] + twin)

    def send_lines(*route, ready=None):
        @pl.loop(1, 16)
        def _(line):
            step_x, step_y = line // 4, lax.rem(line, 4)
            if ready is not None:
                ready(lax.rem(4 - step_x, 4) * 4 + lax.rem(4 - step_y, 4))
            for step_core in range(2):
                place = beside(step_x, step_y, step_core)
                for step in RING:
                    send(*route, ring[step] + place)

    def all_in(incoming, part, in_sem):
        pltpu.make_async_copy(incoming.at[part], incoming.at[part], in_sem.at[part]).wait()

    def all_out(outgoing, part, out_sem):
        span = outgoing.at[part, pl.ds(0, DEVICES - 1)]
        pltpu.make_async_copy(span, span, out_sem.at[part]).wait()

    pack(0)
    pack(1)
    pl.semaphore_wait(barrier, 30)

    @pl.loop(1, 16, unroll=5)
    def _(line):
        greet(cross_sem.at[line], ring[0] + beside(line // 4, lax.rem(line, 4), 0))

    for part in range(PARTS):
        send_own_line(sent, landed, part, send_sem, recv_sem)
    send_lines(sent, landed, 0, send_sem, recv_sem, ready=lambda line: pl.semaphore_wait(cross_sem.at[line], 1))
    send_lines(sent, landed, 1, send_sem, recv_sem)

    table_load.wait()
    split[0], split[1] = halves(table[pl.ds(0, 1536)])

    def twisted(real, imag, sign):
        turn_real, turn_imag = table[pl.ds(1536, DEVICES), :TOKENS], sign * table[pl.ds(1536, DEVICES), TOKENS:]
        return real * turn_real - imag * turn_imag, real * turn_imag + imag * turn_real

    def triple(value, lines):
        high, below = halves(value)
        tables = [split[0, lines], split[0, lines], split[1, lines]]
        return one_dot(jnp.concatenate([high, below, high], axis=1), jnp.concatenate(tables, axis=0))

    @pl.loop(0, PARTS)
    def _(part):
        all_in(landed, part, recv_sem)
        rows[...] = landed[part].astype(F32).reshape(ROWS, TOKENS)
        columns = jnp.concatenate(
            [rows[pl.ds(line, DEVICES, stride=LINES), :].astype(BF16) for line in range(LINES)], axis=1
        )
        stage = one_dot(
            jnp.concatenate([split[0, 0:512], split[1, 0:512]], axis=1), jnp.concatenate([columns, columns], axis=0)
        )
        freq = []
        for line in range(LINES):
            lanes = slice(line * TOKENS, (line + 1) * TOKENS)
            real, imag = twisted(stage[:DEVICES, lanes], stage[DEVICES:, lanes], 1.0)
            spectrum = triple(jnp.concatenate([real, imag], axis=1), slice(512, 768))
            freq.append((spectrum[:, :TOKENS], spectrum[:, TOKENS:]))
        pieces = []
        for which in range(3):
            for held in range(HELD):
                taps_freq, source_freq, signal_freq = (freq[array * HELD + held] for array in range(3))
                one, two = ((taps_freq, source_freq), (taps_freq, signal_freq), (source_freq, signal_freq))[which]
                if which == 0:
                    real = one[0] * two[0] - one[1] * two[1]
                    imag = one[0] * two[1] + one[1] * two[0]
                else:
                    real = one[0] * two[0] + one[1] * two[1]
                    imag = one[0] * two[1] - one[1] * two[0]
                spread = triple(jnp.concatenate([real, imag], axis=1), slice(768, 1024))
                pieces.append(twisted(spread[:, :TOKENS], spread[:, TOKENS:], -1.0))
        tables, values = [], []
        for side in range(2):
            high, below = halves(jnp.concatenate([piece[side] for piece in pieces], axis=1))
            lines = slice(1024 + side * DEVICES, 1280 + side * DEVICES)
            tables += [split[0, lines], split[0, lines], split[1, lines]]
            values += [high, below, high]
        final = one_dot(jnp.concatenate(tables, axis=1), jnp.concatenate(values, axis=0))
        for line in range(LINES):
            result[pl.ds(line, DEVICES, stride=LINES), :] = final[:, line * TOKENS:(line + 1) * TOKENS]
        returned[part] = result[...].reshape(DEVICES, 3, HELD, TOKENS).astype(BF16)
        send_own_line(returned, returned_in, part, return_sem, back_sem)
        send_lines(returned, returned_in, part, return_sem, back_sem)

    for part in range(PARTS):
        all_in(returned_in, part, back_sem)
        lines = pl.ds(part * SLAB, SLAB)
        convolved, back_signal, taps_grad = (
            returned_in[part, :, which].astype(F32).reshape(SLAB, TOKENS) for which in range(3)
        )
        out[0, lines] = (grad[lines].astype(F32) * convolved).astype(BF16)
        out[1, lines] = (back_signal * value[lines].astype(F32)).astype(BF16)
        out[2, lines] = (back_signal * key[lines].astype(F32)).astype(BF16)
        out[3, lines] = taps_grad.astype(BF16)
    for part in range(PARTS):
        all_out(sent, part, send_sem)
        all_out(returned, part, return_sem)


def deal(stacked, grad_query, grad_key, grad_value, grad_filter, sems):
    copies = [
        pltpu.make_async_copy(stacked.at[place], target, sems.at[place])
        for place, target in enumerate((grad_query, grad_key, grad_value, grad_filter))
    ]
    for copy in copies:
        copy.start()
    for copy in copies:
        copy.wait()


def on_device(query_proj, key_proj, value_proj, filter_taps, grad_out):
    table = make_tables()
    block = (CHANNELS, TOKENS)
    packed = (PARTS, DEVICES, 3, HELD, TOKENS)
    operands = [
        pltpu.with_memory_space_constraint(operand, pltpu.HBM)
        for operand in (query_proj, key_proj, value_proj, filter_taps, grad_out, jnp.asarray(table))
    ]
    stacked = pl.pallas_call(
        kernel,
        out_shape=pltpu.VMEM((4,) + block, BF16),
        in_specs=[pl.BlockSpec(memory_space=pltpu.HBM)] * 6,
        out_specs=pl.BlockSpec(memory_space=pltpu.VMEM),
        scratch_shapes=[pltpu.VMEM(block, BF16)] * 5
        + [
            pltpu.VMEM(table.shape, F32),
            pltpu.VMEM((2, 1536, DEVICES), BF16),
            pltpu.VMEM(packed, BF16),
            pltpu.VMEM(packed, BF16),
            pltpu.VMEM((ROWS, TOKENS), F32),
            pltpu.VMEM((ROWS, TOKENS), F32),
            pltpu.VMEM(packed, BF16),
            pltpu.VMEM(packed, BF16),
            pltpu.SemaphoreType.DMA((PARTS, 6)),
            pltpu.SemaphoreType.DMA((PARTS,)),
            pltpu.SemaphoreType.DMA((PARTS,)),
            pltpu.SemaphoreType.DMA((PARTS,)),
            pltpu.SemaphoreType.DMA((PARTS,)),
            pltpu.SemaphoreType.REGULAR((16,)),
        ],
        compiler_params=pltpu.CompilerParams(
            collective_id=0, has_side_effects=True, vmem_limit_bytes=40 * 2**20
        ),
        name="transform_and_exchange",
    )(*operands)
    return pl.pallas_call(
        deal,
        out_shape=[jax.ShapeDtypeStruct(block, BF16)] * 4,
        in_specs=[pl.BlockSpec(memory_space=pltpu.VMEM)],
        out_specs=[pl.BlockSpec(memory_space=pltpu.HBM)] * 4,
        scratch_shapes=[pltpu.SemaphoreType.DMA((4,))],
        name="gate_results",
    )(pltpu.with_memory_space_constraint(stacked, pltpu.VMEM))


def solution(mesh):
    spec = P(None, ("dp", "ctx"))
    return jax.shard_map(on_device, mesh=mesh, in_specs=(spec,) * 5, out_specs=(spec,) * 4, check_vma=False)
```

```python
import jax
import jax.numpy as jnp
import numpy as np
from jax import lax
from jax.experimental import pallas as pl
from jax.experimental.pallas import tpu as pltpu
from jax.sharding import PartitionSpec as P

LOGICAL = pl.DeviceIdType.LOGICAL
DEVICES = 256
INNER = 64
TOKENS = 128
CHANNELS = 1024
PARTS = 2
HELD = CHANNELS // DEVICES // PARTS
LINES = 3 * HELD
ROWS = LINES * DEVICES
SLAB = CHANNELS // PARTS
RING = (4, 3, 5, 2, 6, 1, 7, 0)
FAR, NEAR = RING[:5], RING[5:]
TURNS = (2, 1, 3, 0)
LINES_BY_HOPS = sorted(
    ((x, y) for x in range(4) for y in range(4) if x or y), key=lambda line: -sum(min(step, 4 - step) for step in line)
)
BF16 = jnp.bfloat16
F32 = jnp.float32


def make_tables():
    length = DEVICES * TOKENS
    outer = np.arange(DEVICES)
    inner = np.arange(TOKENS)
    theta = 2.0 * np.pi * (outer[:, None] + 0.25) * outer[None, :] / DEVICES
    cosine, sine = np.cos(theta), -np.sin(theta)
    phase = 2.0 * np.pi * (outer[:, None] + 0.25) * inner[None, :] / length
    twist = np.concatenate([np.cos(phase), -np.sin(phase)], axis=1)
    turn = 2.0 * np.pi * ((inner[:, None] * inner[None, :]) % TOKENS) / TOKENS
    there = np.block([[np.cos(turn), -np.sin(turn)], [np.sin(turn), np.cos(turn)]])
    back = np.block([[np.cos(turn), np.sin(turn)], [-np.sin(turn), np.cos(turn)]])
    stacked = [cosine, sine, there, back, cosine.T / length, sine.T / length, twist]
    return np.concatenate(stacked, axis=0).astype(np.float32)


def one_dot(left, right):
    return jnp.dot(left, right, preferred_element_type=F32)


def halves(value):
    high = value.astype(BF16)
    return high, (value - high.astype(F32)).astype(BF16)


def kernel(
    query_hbm, key_hbm, value_hbm, taps_hbm, grad_hbm, table_hbm, out,
    query, key, value, taps, grad, table, split, sent, landed, rows, result, returned, returned_in,
    load_sem, send_sem, recv_sem, return_sem, back_sem, cross_sem,
):
    me = lax.axis_index("dp") * INNER + lax.axis_index("ctx")
    low = lax.rem(me, 32)
    column = low // 8
    row = lax.rem(low // 2, 4)
    core = lax.rem(low, 2)
    ring = [lax.rem(me // 32 + step, 8) * 32 for step in range(8)]

    columns = [lax.rem(column + step, 4) * 8 for step in range(4)]
    rows_of = [lax.rem(row + step, 4) * 2 for step in range(4)]
    cores = [core, 1 - core]
    twin = columns[0] + rows_of[0] + cores[1]

    loads = []
    for part in range(PARTS):
        lines = pl.ds(part * SLAB, SLAB)
        group = []
        for place, (source, target) in enumerate((
            (taps_hbm, taps), (key_hbm, key), (value_hbm, value), (grad_hbm, grad), (query_hbm, query),
        )):
            copy = pltpu.make_async_copy(source.at[lines], target.at[lines], load_sem.at[part, place])
            copy.start()
            group.append(copy)
        loads.append(group)
    barrier = pltpu.get_barrier_semaphore()

    def greet(semaphore, device):
        pl.semaphore_signal(semaphore, inc=1, device_id=device, device_id_type=LOGICAL)

    def greet_lines(semaphore):
        for x, y in LINES_BY_HOPS:
            greet(semaphore(x * 4 + y), ring[0] + columns[x] + rows_of[y] + core)

    for step in FAR:
        greet(barrier, ring[step] + low)
        greet(barrier, ring[step] + twin)
    greet_lines(lambda line: barrier)
    for step in NEAR:
        if step:
            greet(barrier, ring[step] + low)
        greet(barrier, ring[step] + twin)

    table_load = pltpu.make_async_copy(table_hbm, table, load_sem.at[0, 5])
    table_load.start()

    def pack(part):
        for copy in loads[part]:
            copy.wait()
        lines = pl.ds(part * SLAB, SLAB)
        shape = (DEVICES, HELD, TOKENS)
        sent[part, :, 0] = taps[lines].astype(F32).reshape(shape).astype(BF16)
        sent[part, :, 1] = (key[lines].astype(F32) * value[lines].astype(F32)).reshape(shape).astype(BF16)
        sent[part, :, 2] = (grad[lines].astype(F32) * query[lines].astype(F32)).reshape(shape).astype(BF16)

    def send(outgoing, incoming, part, out_sem, in_sem, device):
        pltpu.make_async_remote_copy(
            src_ref=outgoing.at[part, device],
            dst_ref=incoming.at[part, me],
            send_sem=out_sem.at[part],
            recv_sem=in_sem.at[part],
            device_id=device,
            device_id_type=LOGICAL,
        ).start()

    def keep_own(outgoing, incoming, part, _, in_sem):
        pltpu.make_async_copy(outgoing.at[part, me], incoming.at[part, me], in_sem.at[part]).start()

    def send_own_line(*route):
        for step in RING:
            if step:
                send(*route, ring[step] + low)
            send(*route, ring[step] + twin)

    def send_lines(*route, own):
        for steps in (FAR, NEAR):

            @pl.loop(0, 4)
            def _(turn):
                place_x = lax.rem(column + 2 + turn, 4) * 8
                for y in TURNS:
                    def line():
                        for place_core in cores:
                            for step in steps:
                                if step or y or place_core is not core:
                                    send(*route, ring[step] + place_x + rows_of[y] + place_core)
                    if y or own:
                        line()
                    else:
                        pl.when(turn != 2)(line)
                if NEAR == steps:
                    @pl.when(turn != 2)
                    def _():
                        send(*route, ring[0] + place_x + rows_of[0] + core)

    my_plane = me // 32

    def send_planes(*route, groups):
        for planes in groups:

            @pl.loop(0, 4)
            def _(turn):
                step_x = lax.rem(2 + turn, 4)
                place_x = lax.rem(column + step_x, 4) * 8
                for y in TURNS:
                    for twin_step in range(2):
                        place = place_x + rows_of[y] + cores[twin_step]
                        for plane in planes:
                            if y or twin_step:
                                send(*route, plane * 32 + place)
                            else:

                                @pl.when(jnp.logical_or(step_x != 0, my_plane != plane))
                                def _():
                                    send(*route, plane * 32 + place)

    def all_in(incoming, part, in_sem):
        pltpu.make_async_copy(incoming.at[part], incoming.at[part], in_sem.at[part]).wait()

    def all_out(outgoing, part, out_sem):
        span = outgoing.at[part, pl.ds(0, DEVICES - 1)]
        pltpu.make_async_copy(span, span, out_sem.at[part]).wait()

    pack(0)
    pack(1)
    pl.semaphore_wait(barrier, 30)

    greet_lines(lambda line: cross_sem.at[line])

    def send_when_ready(step_x, place_x, y):
        pl.semaphore_wait(cross_sem.at[lax.rem(4 - step_x, 4) * 4 + (4 - y) % 4], 1)
        for place_core in cores:
            for step in RING:
                send(sent, landed, 0, send_sem, recv_sem, ring[step] + place_x + rows_of[y] + place_core)

    for part in range(PARTS):
        keep_own(sent, landed, part, send_sem, recv_sem)
    send_own_line(sent, landed, 0, send_sem, recv_sem)
    for x, y in [(0, 2), (1, 1), (1, 3), (2, 0), (3, 1), (3, 3), (1, 2), (2, 1), (2, 3), (3, 2), (2, 2), (0, 1), (0, 3), (1, 0), (3, 0)]:
        send_when_ready(x, columns[x], y)
    all_out(sent, 0, send_sem)
    send_lines(sent, landed, 1, send_sem, recv_sem, own=True)

    table_load.wait()
    split[0], split[1] = halves(table[pl.ds(0, 1536)])

    def twisted(real, imag, sign):
        turn_real, turn_imag = table[pl.ds(1536, DEVICES), :TOKENS], sign * table[pl.ds(1536, DEVICES), TOKENS:]
        return real * turn_real - imag * turn_imag, real * turn_imag + imag * turn_real

    def triple(value, lines):
        high, below = halves(value)
        tables = [split[0, lines], split[0, lines], split[1, lines]]
        return one_dot(jnp.concatenate([high, below, high], axis=1), jnp.concatenate(tables, axis=0))

    @pl.loop(0, PARTS)
    def _(part):
        all_in(landed, part, recv_sem)
        rows[...] = landed[part].astype(F32).reshape(ROWS, TOKENS)
        columns = jnp.concatenate(
            [rows[pl.ds(line, DEVICES, stride=LINES), :].astype(BF16) for line in range(LINES)], axis=1
        )
        stage = one_dot(
            jnp.concatenate([split[0, 0:512], split[1, 0:512]], axis=1), jnp.concatenate([columns, columns], axis=0)
        )
        freq = []
        for line in range(LINES):
            lanes = slice(line * TOKENS, (line + 1) * TOKENS)
            real, imag = twisted(stage[:DEVICES, lanes], stage[DEVICES:, lanes], 1.0)
            spectrum = triple(jnp.concatenate([real, imag], axis=1), slice(512, 768))
            freq.append((spectrum[:, :TOKENS], spectrum[:, TOKENS:]))
        pieces = []
        for which in range(3):
            for held in range(HELD):
                taps_freq, source_freq, signal_freq = (freq[array * HELD + held] for array in range(3))
                one, two = ((taps_freq, source_freq), (taps_freq, signal_freq), (source_freq, signal_freq))[which]
                if which == 0:
                    real = one[0] * two[0] - one[1] * two[1]
                    imag = one[0] * two[1] + one[1] * two[0]
                else:
                    real = one[0] * two[0] + one[1] * two[1]
                    imag = one[0] * two[1] - one[1] * two[0]
                spread = triple(jnp.concatenate([real, imag], axis=1), slice(768, 1024))
                pieces.append(twisted(spread[:, :TOKENS], spread[:, TOKENS:], -1.0))
        tables, values = [], []
        for side in range(2):
            high, below = halves(jnp.concatenate([piece[side] for piece in pieces], axis=1))
            lines = slice(1024 + side * DEVICES, 1280 + side * DEVICES)
            tables += [split[0, lines], split[0, lines], split[1, lines]]
            values += [high, below, high]
        final = one_dot(jnp.concatenate(tables, axis=1), jnp.concatenate(values, axis=0))
        for line in range(LINES):
            result[pl.ds(line, DEVICES, stride=LINES), :] = final[:, line * TOKENS:(line + 1) * TOKENS]
        returned[part] = result[...].reshape(DEVICES, 3, HELD, TOKENS).astype(BF16)
        keep_own(returned, returned_in, part, return_sem, back_sem)
        @pl.when(part == 0)
        def _():
            send_planes(returned, returned_in, part, return_sem, back_sem, groups=((0, 1, 2, 3, 4, 5, 6, 7),))

        @pl.when(part == 1)
        def _():
            send_planes(returned, returned_in, part, return_sem, back_sem, groups=((0,), (1,), (2,), (3,), (4, 6), (5, 7)))

    for part in range(PARTS):
        all_in(returned_in, part, back_sem)
        lines = pl.ds(part * SLAB, SLAB)
        convolved, back_signal, taps_grad = (
            returned_in[part, :, which].astype(F32).reshape(SLAB, TOKENS) for which in range(3)
        )
        out[0, lines] = (grad[lines].astype(F32) * convolved).astype(BF16)
        out[1, lines] = (back_signal * value[lines].astype(F32)).astype(BF16)
        out[2, lines] = (back_signal * key[lines].astype(F32)).astype(BF16)
        out[3, lines] = taps_grad.astype(BF16)
    all_out(sent, 1, send_sem)
    for part in range(PARTS):
        all_out(returned, part, return_sem)


def deal(stacked, grad_query, grad_key, grad_value, grad_filter, sems):
    copies = [
        pltpu.make_async_copy(stacked.at[place], target, sems.at[place])
        for place, target in enumerate((grad_query, grad_key, grad_value, grad_filter))
    ]
    for copy in copies:
        copy.start()
    for copy in copies:
        copy.wait()


def on_device(query_proj, key_proj, value_proj, filter_taps, grad_out):
    table = make_tables()
    block = (CHANNELS, TOKENS)
    packed = (PARTS, DEVICES, 3, HELD, TOKENS)
    operands = [
        pltpu.with_memory_space_constraint(operand, pltpu.HBM)
        for operand in (query_proj, key_proj, value_proj, filter_taps, grad_out, jnp.asarray(table))
    ]
    stacked = pl.pallas_call(
        kernel,
        out_shape=pltpu.VMEM((4,) + block, BF16),
        in_specs=[pl.BlockSpec(memory_space=pltpu.HBM)] * 6,
        out_specs=pl.BlockSpec(memory_space=pltpu.VMEM),
        scratch_shapes=[pltpu.VMEM(block, BF16)] * 5
        + [
            pltpu.VMEM(table.shape, F32),
            pltpu.VMEM((2, 1536, DEVICES), BF16),
            pltpu.VMEM(packed, BF16),
            pltpu.VMEM(packed, BF16),
            pltpu.VMEM((ROWS, TOKENS), F32),
            pltpu.VMEM((ROWS, TOKENS), F32),
            pltpu.VMEM(packed, BF16),
            pltpu.VMEM(packed, BF16),
            pltpu.SemaphoreType.DMA((PARTS, 6)),
            pltpu.SemaphoreType.DMA((PARTS,)),
            pltpu.SemaphoreType.DMA((PARTS,)),
            pltpu.SemaphoreType.DMA((PARTS,)),
            pltpu.SemaphoreType.DMA((PARTS,)),
            pltpu.SemaphoreType.REGULAR((16,)),
        ],
        compiler_params=pltpu.CompilerParams(
            collective_id=0, has_side_effects=True, vmem_limit_bytes=40 * 2**20
        ),
        name="transform_and_exchange",
    )(*operands)
    return pl.pallas_call(
        deal,
        out_shape=[jax.ShapeDtypeStruct(block, BF16)] * 4,
        in_specs=[pl.BlockSpec(memory_space=pltpu.VMEM)],
        out_specs=[pl.BlockSpec(memory_space=pltpu.HBM)] * 4,
        scratch_shapes=[pltpu.SemaphoreType.DMA((4,))],
        name="gate_results",
    )(pltpu.with_memory_space_constraint(stacked, pltpu.VMEM))


def solution(mesh):
    spec = P(None, ("dp", "ctx"))
    return jax.shard_map(on_device, mesh=mesh, in_specs=(spec,) * 5, out_specs=(spec,) * 4, check_vma=False)
```

```python
import jax
import jax.numpy as jnp
import numpy as np
from jax import lax
from jax.experimental import pallas as pl
from jax.experimental.pallas import tpu as pltpu
from jax.sharding import PartitionSpec as P

LOGICAL = pl.DeviceIdType.LOGICAL
DEVICES = 256
INNER = 64
TOKENS = 128
CHANNELS = 1024
PARTS = 2
HELD = CHANNELS // DEVICES // PARTS
LINES = 3 * HELD
ROWS = LINES * DEVICES
SLAB = CHANNELS // PARTS
RING = (4, 3, 5, 2, 6, 1, 7, 0)
FAR, NEAR = RING[:5], RING[5:]
TURNS = (2, 1, 3, 0)
LINES_BY_HOPS = sorted(
    ((x, y) for x in range(4) for y in range(4) if x or y), key=lambda line: -sum(min(step, 4 - step) for step in line)
)
BF16 = jnp.bfloat16
F32 = jnp.float32


def make_tables():
    length = DEVICES * TOKENS
    outer = np.arange(DEVICES)
    inner = np.arange(TOKENS)
    theta = 2.0 * np.pi * (outer[:, None] + 0.25) * outer[None, :] / DEVICES
    cosine, sine = np.cos(theta), -np.sin(theta)
    phase = 2.0 * np.pi * (outer[:, None] + 0.25) * inner[None, :] / length
    twist = np.concatenate([np.cos(phase), -np.sin(phase)], axis=1)
    turn = 2.0 * np.pi * ((inner[:, None] * inner[None, :]) % TOKENS) / TOKENS
    there = np.block([[np.cos(turn), -np.sin(turn)], [np.sin(turn), np.cos(turn)]])
    back = np.block([[np.cos(turn), np.sin(turn)], [-np.sin(turn), np.cos(turn)]])
    stacked = [cosine, sine, there, back, cosine.T / length, sine.T / length, twist]
    return np.concatenate(stacked, axis=0).astype(np.float32)


def one_dot(left, right):
    return jnp.dot(left, right, preferred_element_type=F32)


def halves(value):
    high = value.astype(BF16)
    return high, (value - high.astype(F32)).astype(BF16)


def kernel(
    query_hbm, key_hbm, value_hbm, taps_hbm, grad_hbm, table_hbm, out,
    query, key, value, taps, grad, table, split, sent, landed, rows, result, returned, returned_in,
    load_sem, send_sem, recv_sem, return_sem, back_sem, cross_sem,
):
    me = lax.axis_index("dp") * INNER + lax.axis_index("ctx")
    low = lax.rem(me, 32)
    column = low // 8
    row = lax.rem(low // 2, 4)
    core = lax.rem(low, 2)
    ring = [lax.rem(me // 32 + step, 8) * 32 for step in range(8)]

    columns = [lax.rem(column + step, 4) * 8 for step in range(4)]
    rows_of = [lax.rem(row + step, 4) * 2 for step in range(4)]
    cores = [core, 1 - core]
    twin = columns[0] + rows_of[0] + cores[1]

    loads = []
    for part in range(PARTS):
        lines = pl.ds(part * SLAB, SLAB)
        group = []
        for place, (source, target) in enumerate((
            (taps_hbm, taps), (key_hbm, key), (value_hbm, value), (grad_hbm, grad), (query_hbm, query),
        )):
            copy = pltpu.make_async_copy(source.at[lines], target.at[lines], load_sem.at[part, place])
            copy.start()
            group.append(copy)
        loads.append(group)
    barrier = pltpu.get_barrier_semaphore()

    def greet(semaphore, device):
        pl.semaphore_signal(semaphore, inc=1, device_id=device, device_id_type=LOGICAL)

    def greet_lines(semaphore):
        for x, y in LINES_BY_HOPS:
            greet(semaphore(x * 4 + y), ring[0] + columns[x] + rows_of[y] + core)

    for step in FAR:
        greet(barrier, ring[step] + low)
        greet(barrier, ring[step] + twin)
    greet_lines(lambda line: barrier)
    for step in NEAR:
        if step:
            greet(barrier, ring[step] + low)
        greet(barrier, ring[step] + twin)

    table_load = pltpu.make_async_copy(table_hbm, table, load_sem.at[0, 5])
    table_load.start()

    def pack(part):
        for copy in loads[part]:
            copy.wait()
        lines = pl.ds(part * SLAB, SLAB)
        shape = (DEVICES, HELD, TOKENS)
        sent[part, :, 0] = taps[lines].astype(F32).reshape(shape).astype(BF16)
        sent[part, :, 1] = (key[lines].astype(F32) * value[lines].astype(F32)).reshape(shape).astype(BF16)
        sent[part, :, 2] = (grad[lines].astype(F32) * query[lines].astype(F32)).reshape(shape).astype(BF16)

    def send(outgoing, incoming, part, out_sem, in_sem, device):
        pltpu.make_async_remote_copy(
            src_ref=outgoing.at[part, device],
            dst_ref=incoming.at[part, me],
            send_sem=out_sem.at[part],
            recv_sem=in_sem.at[part],
            device_id=device,
            device_id_type=LOGICAL,
        ).start()

    def keep_own(outgoing, incoming, part, _, in_sem):
        pltpu.make_async_copy(outgoing.at[part, me], incoming.at[part, me], in_sem.at[part]).start()

    def send_own_line(*route):
        for step in RING:
            if step:
                send(*route, ring[step] + low)
            send(*route, ring[step] + twin)

    def send_lines(*route, own):
        for steps in (FAR, NEAR):

            @pl.loop(0, 4)
            def _(turn):
                place_x = lax.rem(column + 2 + turn, 4) * 8
                for y in TURNS:
                    def line():
                        for place_core in cores:
                            for step in steps:
                                if step or y or place_core is not core:
                                    send(*route, ring[step] + place_x + rows_of[y] + place_core)
                    if y or own:
                        line()
                    else:
                        pl.when(turn != 2)(line)
                if NEAR == steps:
                    @pl.when(turn != 2)
                    def _():
                        send(*route, ring[0] + place_x + rows_of[0] + core)

    def send_planes(*route, groups):
        for planes in groups:

            @pl.loop(0, 4)
            def _(place_x):
                for y in range(4):
                    for place_core in (1, 0):
                        for plane in planes:
                            device = plane * 32 + place_x * 8 + y * 2 + place_core

                            @pl.when(device != me)
                            def _():
                                send(*route, device)

    def all_in(incoming, part, in_sem):
        pltpu.make_async_copy(incoming.at[part], incoming.at[part], in_sem.at[part]).wait()

    def all_out(outgoing, part, out_sem):
        span = outgoing.at[part, pl.ds(0, DEVICES - 1)]
        pltpu.make_async_copy(span, span, out_sem.at[part]).wait()

    pack(0)
    pack(1)
    pl.semaphore_wait(barrier, 30)

    greet_lines(lambda line: cross_sem.at[line])

    def send_when_ready(step_x, place_x, y):
        pl.semaphore_wait(cross_sem.at[lax.rem(4 - step_x, 4) * 4 + (4 - y) % 4], 1)
        for place_core in cores:
            for step in RING:
                send(sent, landed, 0, send_sem, recv_sem, ring[step] + place_x + rows_of[y] + place_core)

    for part in range(PARTS):
        keep_own(sent, landed, part, send_sem, recv_sem)
    send_own_line(sent, landed, 0, send_sem, recv_sem)
    for x, y in [(0, 2), (1, 1), (1, 3), (2, 0), (3, 1), (3, 3), (1, 2), (2, 1), (2, 3), (3, 2), (2, 2), (0, 1), (0, 3), (1, 0), (3, 0)]:
        send_when_ready(x, columns[x], y)
    all_out(sent, 0, send_sem)
    send_lines(sent, landed, 1, send_sem, recv_sem, own=True)

    table_load.wait()
    split[0], split[1] = halves(table[pl.ds(0, 1536)])

    def twisted(real, imag, sign):
        turn_real, turn_imag = table[pl.ds(1536, DEVICES), :TOKENS], sign * table[pl.ds(1536, DEVICES), TOKENS:]
        return real * turn_real - imag * turn_imag, real * turn_imag + imag * turn_real

    def triple(value, lines):
        high, below = halves(value)
        tables = [split[0, lines], split[0, lines], split[1, lines]]
        return one_dot(jnp.concatenate([high, below, high], axis=1), jnp.concatenate(tables, axis=0))

    @pl.loop(0, PARTS)
    def _(part):
        all_in(landed, part, recv_sem)
        rows[...] = landed[part].astype(F32).reshape(ROWS, TOKENS)
        columns = jnp.concatenate(
            [rows[pl.ds(line, DEVICES, stride=LINES), :].astype(BF16) for line in range(LINES)], axis=1
        )
        stage = one_dot(
            jnp.concatenate([split[0, 0:512], split[1, 0:512]], axis=1), jnp.concatenate([columns, columns], axis=0)
        )
        freq = []
        for line in range(LINES):
            lanes = slice(line * TOKENS, (line + 1) * TOKENS)
            real, imag = twisted(stage[:DEVICES, lanes], stage[DEVICES:, lanes], 1.0)
            spectrum = triple(jnp.concatenate([real, imag], axis=1), slice(512, 768))
            freq.append((spectrum[:, :TOKENS], spectrum[:, TOKENS:]))
        pieces = []
        for which in range(3):
            for held in range(HELD):
                taps_freq, source_freq, signal_freq = (freq[array * HELD + held] for array in range(3))
                one, two = ((taps_freq, source_freq), (taps_freq, signal_freq), (source_freq, signal_freq))[which]
                if which == 0:
                    real = one[0] * two[0] - one[1] * two[1]
                    imag = one[0] * two[1] + one[1] * two[0]
                else:
                    real = one[0] * two[0] + one[1] * two[1]
                    imag = one[0] * two[1] - one[1] * two[0]
                spread = triple(jnp.concatenate([real, imag], axis=1), slice(768, 1024))
                pieces.append(twisted(spread[:, :TOKENS], spread[:, TOKENS:], -1.0))
        tables, values = [], []
        for side in range(2):
            high, below = halves(jnp.concatenate([piece[side] for piece in pieces], axis=1))
            lines = slice(1024 + side * DEVICES, 1280 + side * DEVICES)
            tables += [split[0, lines], split[0, lines], split[1, lines]]
            values += [high, below, high]
        final = one_dot(jnp.concatenate(tables, axis=1), jnp.concatenate(values, axis=0))
        for line in range(LINES):
            result[pl.ds(line, DEVICES, stride=LINES), :] = final[:, line * TOKENS:(line + 1) * TOKENS]
        returned[part] = result[...].reshape(DEVICES, 3, HELD, TOKENS).astype(BF16)
        keep_own(returned, returned_in, part, return_sem, back_sem)
        @pl.when(part == 0)
        def _():
            send_planes(returned, returned_in, part, return_sem, back_sem, groups=((0, 1, 2, 3, 4, 5, 6, 7),))

        @pl.when(part == 1)
        def _():
            send_planes(returned, returned_in, part, return_sem, back_sem, groups=((0,), (1, 2), (3,), (4, 6), (5, 7)))

    for part in range(PARTS):
        all_in(returned_in, part, back_sem)
        lines = pl.ds(part * SLAB, SLAB)
        convolved, back_signal, taps_grad = (
            returned_in[part, :, which].astype(F32).reshape(SLAB, TOKENS) for which in range(3)
        )
        out[0, lines] = (grad[lines].astype(F32) * convolved).astype(BF16)
        out[1, lines] = (back_signal * value[lines].astype(F32)).astype(BF16)
        out[2, lines] = (back_signal * key[lines].astype(F32)).astype(BF16)
        out[3, lines] = taps_grad.astype(BF16)
    all_out(sent, 1, send_sem)
    for part in range(PARTS):
        all_out(returned, part, return_sem)


def deal(stacked, grad_query, grad_key, grad_value, grad_filter, sems):
    copies = [
        pltpu.make_async_copy(stacked.at[place], target, sems.at[place])
        for place, target in enumerate((grad_query, grad_key, grad_value, grad_filter))
    ]
    for copy in copies:
        copy.start()
    for copy in copies:
        copy.wait()


def on_device(query_proj, key_proj, value_proj, filter_taps, grad_out):
    table = make_tables()
    block = (CHANNELS, TOKENS)
    packed = (PARTS, DEVICES, 3, HELD, TOKENS)
    operands = [
        pltpu.with_memory_space_constraint(operand, pltpu.HBM)
        for operand in (query_proj, key_proj, value_proj, filter_taps, grad_out, jnp.asarray(table))
    ]
    stacked = pl.pallas_call(
        kernel,
        out_shape=pltpu.VMEM((4,) + block, BF16),
        in_specs=[pl.BlockSpec(memory_space=pltpu.HBM)] * 6,
        out_specs=pl.BlockSpec(memory_space=pltpu.VMEM),
        scratch_shapes=[pltpu.VMEM(block, BF16)] * 5
        + [
            pltpu.VMEM(table.shape, F32),
            pltpu.VMEM((2, 1536, DEVICES), BF16),
            pltpu.VMEM(packed, BF16),
            pltpu.VMEM(packed, BF16),
            pltpu.VMEM((ROWS, TOKENS), F32),
            pltpu.VMEM((ROWS, TOKENS), F32),
            pltpu.VMEM(packed, BF16),
            pltpu.VMEM(packed, BF16),
            pltpu.SemaphoreType.DMA((PARTS, 6)),
            pltpu.SemaphoreType.DMA((PARTS,)),
            pltpu.SemaphoreType.DMA((PARTS,)),
            pltpu.SemaphoreType.DMA((PARTS,)),
            pltpu.SemaphoreType.DMA((PARTS,)),
            pltpu.SemaphoreType.REGULAR((16,)),
        ],
        compiler_params=pltpu.CompilerParams(
            collective_id=0, has_side_effects=True, vmem_limit_bytes=40 * 2**20
        ),
        name="transform_and_exchange",
    )(*operands)
    return pl.pallas_call(
        deal,
        out_shape=[jax.ShapeDtypeStruct(block, BF16)] * 4,
        in_specs=[pl.BlockSpec(memory_space=pltpu.VMEM)],
        out_specs=[pl.BlockSpec(memory_space=pltpu.HBM)] * 4,
        scratch_shapes=[pltpu.SemaphoreType.DMA((4,))],
        name="gate_results",
    )(pltpu.with_memory_space_constraint(stacked, pltpu.VMEM))


def solution(mesh):
    spec = P(None, ("dp", "ctx"))
    return jax.shard_map(on_device, mesh=mesh, in_specs=(spec,) * 5, out_specs=(spec,) * 4, check_vma=False)
```

```python
import jax
import jax.numpy as jnp
import numpy as np
from jax import lax
from jax.experimental import pallas as pl
from jax.experimental.pallas import tpu as pltpu
from jax.sharding import PartitionSpec as P

LOGICAL = pl.DeviceIdType.LOGICAL
DEVICES = 256
INNER = 64
HALF = DEVICES // 2
TOKENS = 128
CHANNELS = 1024
PARTS = 2
HELD = CHANNELS // DEVICES // PARTS
LINES = 3 * HELD
ROWS = LINES * DEVICES
SLAB = CHANNELS // PARTS
RING = (4, 3, 5, 2, 6, 1, 7, 0)
FAR, NEAR = RING[:5], RING[5:]
TURNS = (2, 1, 3, 0)
LINES_BY_HOPS = sorted(
    ((x, y) for x in range(4) for y in range(4) if x or y), key=lambda line: -sum(min(step, 4 - step) for step in line)
)
BF16 = jnp.bfloat16
F32 = jnp.float32


def make_tables():
    length = DEVICES * TOKENS
    outer = np.arange(DEVICES)
    inner = np.arange(TOKENS)
    theta = 2.0 * np.pi * (outer[:, None] + 0.25) * outer[None, :] / DEVICES
    cosine, sine = np.cos(theta), -np.sin(theta)
    phase = 2.0 * np.pi * (outer[:, None] + 0.25) * inner[None, :] / length
    twist = np.concatenate([np.cos(phase), -np.sin(phase)], axis=1)
    turn = 2.0 * np.pi * ((inner[:, None] * inner[None, :]) % TOKENS) / TOKENS
    there = np.block([[np.cos(turn), -np.sin(turn)], [np.sin(turn), np.cos(turn)]])
    back = np.block([[np.cos(turn), np.sin(turn)], [-np.sin(turn), np.cos(turn)]])
    stacked = [cosine, sine, there, back, cosine.T / length, sine.T / length, twist]
    return np.concatenate(stacked, axis=0).astype(np.float32)


def one_dot(left, right):
    return jnp.dot(left, right, preferred_element_type=F32)


def halves(value):
    high = value.astype(BF16)
    return high, (value - high.astype(F32)).astype(BF16)


def kernel(
    query_hbm, key_hbm, value_hbm, taps_hbm, grad_hbm, table_hbm, out,
    query, key, value, taps, grad, table, split, sent, landed, rows, result, returned, returned_in,
    load_sem, send_sem, recv_sem, return_sem, back_sem, cross_sem,
):
    me = lax.axis_index("dp") * INNER + lax.axis_index("ctx")
    low = lax.rem(me, 32)
    column = low // 8
    row = lax.rem(low // 2, 4)
    core = lax.rem(low, 2)
    ring = [lax.rem(me // 32 + step, 8) * 32 for step in range(8)]

    columns = [lax.rem(column + step, 4) * 8 for step in range(4)]
    rows_of = [lax.rem(row + step, 4) * 2 for step in range(4)]
    cores = [core, 1 - core]
    twin = columns[0] + rows_of[0] + cores[1]

    loads = []
    for part in range(PARTS):
        lines = pl.ds(part * SLAB, SLAB)
        group = []
        for place, (source, target) in enumerate((
            (taps_hbm, taps), (key_hbm, key), (value_hbm, value), (grad_hbm, grad), (query_hbm, query),
        )):
            copy = pltpu.make_async_copy(source.at[lines], target.at[lines], load_sem.at[part, place])
            copy.start()
            group.append(copy)
        loads.append(group)
    barrier = pltpu.get_barrier_semaphore()

    def greet(semaphore, device):
        pl.semaphore_signal(semaphore, inc=1, device_id=device, device_id_type=LOGICAL)

    def greet_lines(semaphore):
        for x, y in LINES_BY_HOPS:
            greet(semaphore(x * 4 + y), ring[0] + columns[x] + rows_of[y] + core)

    for step in FAR:
        greet(barrier, ring[step] + low)
        greet(barrier, ring[step] + twin)
    greet_lines(lambda line: barrier)
    for step in NEAR:
        if step:
            greet(barrier, ring[step] + low)
        greet(barrier, ring[step] + twin)

    table_load = pltpu.make_async_copy(table_hbm, table, load_sem.at[0, 5])
    table_load.start()

    def pack(part):
        for copy in loads[part]:
            copy.wait()
        lines = pl.ds(part * SLAB, SLAB)
        shape = (DEVICES, HELD, TOKENS)
        sent[part, :, 0] = taps[lines].astype(F32).reshape(shape).astype(BF16)
        sent[part, :, 1] = (key[lines].astype(F32) * value[lines].astype(F32)).reshape(shape).astype(BF16)
        sent[part, :, 2] = (grad[lines].astype(F32) * query[lines].astype(F32)).reshape(shape).astype(BF16)

    def send(outgoing, incoming, part, out_sem, in_sem, device):
        pltpu.make_async_remote_copy(
            src_ref=outgoing.at[part, device],
            dst_ref=incoming.at[part, me],
            send_sem=out_sem.at[part],
            recv_sem=in_sem,
            device_id=device,
            device_id_type=LOGICAL,
        ).start()

    def keep_own(outgoing, incoming, part, _, in_sem):
        pltpu.make_async_copy(outgoing.at[part, me], incoming.at[part, me], in_sem).start()

    def send_own_line(*route):
        for step in RING:
            if step:
                send(*route, ring[step] + low)
            send(*route, ring[step] + twin)

    def send_lines(*route, own):
        for steps in (FAR, NEAR):

            @pl.loop(0, 4)
            def _(turn):
                place_x = lax.rem(column + 2 + turn, 4) * 8
                for y in TURNS:
                    def line():
                        for place_core in cores:
                            for step in steps:
                                if step or y or place_core is not core:
                                    send(*route, ring[step] + place_x + rows_of[y] + place_core)
                    if y or own:
                        line()
                    else:
                        pl.when(turn != 2)(line)
                if NEAR == steps:
                    @pl.when(turn != 2)
                    def _():
                        send(*route, ring[0] + place_x + rows_of[0] + core)

    def send_planes(*route, groups):
        for planes in groups:

            @pl.loop(0, 4)
            def _(place_x):
                for y in range(4):
                    for place_core in (1, 0):
                        for plane in planes:
                            device = plane * 32 + place_x * 8 + y * 2 + place_core

                            @pl.when(device != me)
                            def _():
                                send(*route, device)

    def all_in(span, in_sem):
        pltpu.make_async_copy(span, span, in_sem).wait()

    def all_out(outgoing, part, out_sem):
        span = outgoing.at[part, pl.ds(0, DEVICES - 1)]
        pltpu.make_async_copy(span, span, out_sem.at[part]).wait()

    pack(0)
    pack(1)
    pl.semaphore_wait(barrier, 30)

    greet_lines(lambda line: cross_sem.at[line])

    def send_when_ready(step_x, place_x, y):
        pl.semaphore_wait(cross_sem.at[lax.rem(4 - step_x, 4) * 4 + (4 - y) % 4], 1)
        for place_core in cores:
            for step in RING:
                send(sent, landed, 0, send_sem, recv_sem.at[0], ring[step] + place_x + rows_of[y] + place_core)

    for part in range(PARTS):
        keep_own(sent, landed, part, send_sem, recv_sem.at[part])
    send_own_line(sent, landed, 0, send_sem, recv_sem.at[0])
    for x, y in [(0, 2), (1, 1), (1, 3), (2, 0), (3, 1), (3, 3), (1, 2), (2, 1), (2, 3), (3, 2), (2, 2), (0, 1), (0, 3), (1, 0), (3, 0)]:
        send_when_ready(x, columns[x], y)
    send_lines(sent, landed, 1, send_sem, recv_sem.at[1], own=True)

    table_load.wait()
    split[0], split[1] = halves(table[pl.ds(0, 1536)])

    def twisted(real, imag, sign):
        turn_real, turn_imag = table[pl.ds(1536, DEVICES), :TOKENS], sign * table[pl.ds(1536, DEVICES), TOKENS:]
        return real * turn_real - imag * turn_imag, real * turn_imag + imag * turn_real

    def triple(value, lines):
        high, below = halves(value)
        tables = [split[0, lines], split[0, lines], split[1, lines]]
        return one_dot(jnp.concatenate([high, below, high], axis=1), jnp.concatenate(tables, axis=0))

    @pl.loop(0, PARTS)
    def _(part):
        all_in(landed.at[part], recv_sem.at[part])
        rows[...] = landed[part].astype(F32).reshape(ROWS, TOKENS)
        columns = jnp.concatenate(
            [rows[pl.ds(line, DEVICES, stride=LINES), :].astype(BF16) for line in range(LINES)], axis=1
        )
        stage = one_dot(
            jnp.concatenate([split[0, 0:512], split[1, 0:512]], axis=1), jnp.concatenate([columns, columns], axis=0)
        )
        freq = []
        for line in range(LINES):
            lanes = slice(line * TOKENS, (line + 1) * TOKENS)
            real, imag = twisted(stage[:DEVICES, lanes], stage[DEVICES:, lanes], 1.0)
            spectrum = triple(jnp.concatenate([real, imag], axis=1), slice(512, 768))
            freq.append((spectrum[:, :TOKENS], spectrum[:, TOKENS:]))
        pieces = []
        for which in range(3):
            for held in range(HELD):
                taps_freq, source_freq, signal_freq = (freq[array * HELD + held] for array in range(3))
                one, two = ((taps_freq, source_freq), (taps_freq, signal_freq), (source_freq, signal_freq))[which]
                if which == 0:
                    real = one[0] * two[0] - one[1] * two[1]
                    imag = one[0] * two[1] + one[1] * two[0]
                else:
                    real = one[0] * two[0] + one[1] * two[1]
                    imag = one[0] * two[1] - one[1] * two[0]
                spread = triple(jnp.concatenate([real, imag], axis=1), slice(768, 1024))
                pieces.append(twisted(spread[:, :TOKENS], spread[:, TOKENS:], -1.0))
        tables, values = [], []
        for side in range(2):
            high, below = halves(jnp.concatenate([piece[side] for piece in pieces], axis=1))
            lines = slice(1024 + side * DEVICES, 1280 + side * DEVICES)
            tables += [split[0, lines], split[0, lines], split[1, lines]]
            values += [high, below, high]
        final = one_dot(jnp.concatenate(tables, axis=1), jnp.concatenate(values, axis=0))
        for line in range(LINES):
            result[pl.ds(line, DEVICES, stride=LINES), :] = final[:, line * TOKENS:(line + 1) * TOKENS]
        returned[part] = result[...].reshape(DEVICES, 3, HELD, TOKENS).astype(BF16)
        keep_own(returned, returned_in, part, return_sem, back_sem.at[part, me // HALF])
        @pl.when(part == 0)
        def _():
            send_planes(returned, returned_in, part, return_sem, back_sem.at[part, me // HALF], groups=((0, 2, 4, 6), (1, 3, 5, 7)))

        @pl.when(part == 1)
        def _():
            send_planes(returned, returned_in, part, return_sem, back_sem.at[part, me // HALF], groups=((0,), (1, 2), (3, 4, 7), (5, 6)))

    for part in range(PARTS):
        for half in range(2):
            all_in(returned_in.at[part, pl.ds(half * HALF, HALF)], back_sem.at[part, half])
            lines = pl.ds(part * SLAB + half * (SLAB // 2), SLAB // 2)
            convolved, back_signal, taps_grad = (
                returned_in[part, pl.ds(half * HALF, HALF), which].astype(F32).reshape(SLAB // 2, TOKENS)
                for which in range(3)
            )
            out[0, lines] = (grad[lines].astype(F32) * convolved).astype(BF16)
            out[1, lines] = (back_signal * value[lines].astype(F32)).astype(BF16)
            out[2, lines] = (back_signal * key[lines].astype(F32)).astype(BF16)
            out[3, lines] = taps_grad.astype(BF16)
    for part in range(PARTS):
        all_out(sent, part, send_sem)
        all_out(returned, part, return_sem)


def deal(stacked, grad_query, grad_key, grad_value, grad_filter, sems):
    copies = [
        pltpu.make_async_copy(stacked.at[place], target, sems.at[place])
        for place, target in enumerate((grad_query, grad_key, grad_value, grad_filter))
    ]
    for copy in copies:
        copy.start()
    for copy in copies:
        copy.wait()


def on_device(query_proj, key_proj, value_proj, filter_taps, grad_out):
    table = make_tables()
    block = (CHANNELS, TOKENS)
    packed = (PARTS, DEVICES, 3, HELD, TOKENS)
    operands = [
        pltpu.with_memory_space_constraint(operand, pltpu.HBM)
        for operand in (query_proj, key_proj, value_proj, filter_taps, grad_out, jnp.asarray(table))
    ]
    stacked = pl.pallas_call(
        kernel,
        out_shape=pltpu.VMEM((4,) + block, BF16),
        in_specs=[pl.BlockSpec(memory_space=pltpu.HBM)] * 6,
        out_specs=pl.BlockSpec(memory_space=pltpu.VMEM),
        scratch_shapes=[pltpu.VMEM(block, BF16)] * 5
        + [
            pltpu.VMEM(table.shape, F32),
            pltpu.VMEM((2, 1536, DEVICES), BF16),
            pltpu.VMEM(packed, BF16),
            pltpu.VMEM(packed, BF16),
            pltpu.VMEM((ROWS, TOKENS), F32),
            pltpu.VMEM((ROWS, TOKENS), F32),
            pltpu.VMEM(packed, BF16),
            pltpu.VMEM(packed, BF16),
            pltpu.SemaphoreType.DMA((PARTS, 6)),
            pltpu.SemaphoreType.DMA((PARTS,)),
            pltpu.SemaphoreType.DMA((PARTS,)),
            pltpu.SemaphoreType.DMA((PARTS,)),
            pltpu.SemaphoreType.DMA((PARTS, 2)),
            pltpu.SemaphoreType.REGULAR((16,)),
        ],
        compiler_params=pltpu.CompilerParams(
            collective_id=0, has_side_effects=True, vmem_limit_bytes=40 * 2**20
        ),
        name="transform_and_exchange",
    )(*operands)
    return pl.pallas_call(
        deal,
        out_shape=[jax.ShapeDtypeStruct(block, BF16)] * 4,
        in_specs=[pl.BlockSpec(memory_space=pltpu.VMEM)],
        out_specs=[pl.BlockSpec(memory_space=pltpu.HBM)] * 4,
        scratch_shapes=[pltpu.SemaphoreType.DMA((4,))],
        name="gate_results",
    )(pltpu.with_memory_space_constraint(stacked, pltpu.VMEM))


def solution(mesh):
    spec = P(None, ("dp", "ctx"))
    return jax.shard_map(on_device, mesh=mesh, in_specs=(spec,) * 5, out_specs=(spec,) * 4, check_vma=False)
```
